32 devices in a mesh: row: 2 (over x), col: 16 (over z, y, core).
Axes of the slice: x: 2, y: 2, z: 4, core: 2. Of those that a mesh axis runs over, the one named last changes fastest.
Arguments:
- blocks: bfloat16 [2, 16, 8, 512, 512], P('row', 'col'), may hold values from -0.046875 to 0.046875
- block_rows: int32 [2, 16, 8], P('row', 'col'), may hold values from 0 to 3, as said below
- block_cols: int32 [2, 16, 8], P('row', 'col'), may hold values from 0 to 3
- sketch: bfloat16 [4096, 32], P('row'), may hold values from -6 to 6
- theta: float32 [32768], P('col'), may hold values from 0.1 to 10
- rhs: float32 [4096], P('row'), may hold values from -6 to 6
Outputs:
- solution: float32 [4096], P(('row', 'col'))
- residual: float32 [4096], P(('row', 'col'))
- precond_residual: float32 [4096], P(('row', 'col'))
The draws below stay inside these ranges and needn't reach their ends.
Inputs may be any that keep to these rules, and one draw needn't show every extreme that they name: Within one tile the pairs (block_rows, block_cols) are all different.
All inputs are finite; a program needn't handle non-finite values.
Results may differ from the reference program's by a relative error of at most 0.005.
Values may be sent and summed in bfloat16 or wider, within the bound.
A program may use at most 64 MiB of HBM per device.

```python
import math
import jax
import jax.numpy as jnp
from jax import lax

BLOCK = 512
SKETCH = 32
ROW_BLOCKS = 4
COL_BLOCKS = 4
TILE_BLOCKS = 8
GRID_ROWS = 2
GRID_COLS = 16
ROWS = 4096
COLUMNS = 32768


def tile_positions(key):
    keys = jax.random.split(key, GRID_ROWS * GRID_COLS)
    chosen = jax.vmap(lambda k: jax.random.permutation(k, ROW_BLOCKS * COL_BLOCKS)[:TILE_BLOCKS])(keys)
    return chosen.reshape(GRID_ROWS, GRID_COLS, TILE_BLOCKS).astype(jnp.int32)


def shared_factors(key):
    pattern_key = jax.random.fold_in(key, 101)
    strength_key = jax.random.fold_in(key, 103)
    alignment_key = jax.random.fold_in(key, 107)
    pattern = jnp.clip(jax.random.normal(pattern_key, (GRID_ROWS, BLOCK), jnp.float32), -2.5, 2.5)
    highest = min(16.0, 0.7 * math.sqrt(BLOCK))
    strength = jnp.exp(jax.random.uniform(strength_key, (GRID_ROWS,), jnp.float32, math.log(highest / 8.0), math.log(highest)))
    alignment = jax.random.uniform(alignment_key, (GRID_ROWS, ROW_BLOCKS), jnp.float32, -1.0, 1.0)
    return (pattern, strength, alignment)


def draw_block_rows(key, part):
    places = tile_positions(key)
    return (places // COL_BLOCKS).astype(jnp.int32)


def draw_block_cols(key, part):
    places = tile_positions(key)
    return (places % COL_BLOCKS).astype(jnp.int32)


def draw_blocks(key, part):
    pattern, strength, alignment = shared_factors(key)
    key = jax.random.fold_in(key, 7)
    noise_key = jax.random.fold_in(key, 1)
    factor_key = jax.random.fold_in(key, 2)
    fan_in = BLOCK * TILE_BLOCKS * GRID_COLS / ROW_BLOCKS
    sigma = 1.0 / math.sqrt(fan_in)
    full_shape = (GRID_ROWS, GRID_COLS, TILE_BLOCKS, BLOCK, BLOCK)
    noise_part = jnp.clip(jax.random.normal(noise_key, full_shape, jnp.float32), -4.0, 4.0)
    factor = jnp.clip(jax.random.normal(factor_key, (GRID_ROWS, GRID_COLS, TILE_BLOCKS, BLOCK), jnp.float32), -2.5, 2.5)
    weight_row = strength / math.sqrt(fan_in * BLOCK)
    coupling = weight_row[:, None, None, None, None] * pattern[:, None, None, :, None] * factor[:, :, :, None, :]
    limit = 5.95 * sigma
    return jnp.clip(sigma * noise_part + coupling, -limit, limit).astype(jnp.bfloat16)


def draw_rhs(key, part):
    pattern, strength, alignment = shared_factors(key)
    key = jax.random.fold_in(key, 9)
    noise_part = jnp.clip(jax.random.normal(key, (GRID_ROWS, ROW_BLOCKS, BLOCK), jnp.float32), -3.4, 3.4)
    aligned = alignment[:, :, None] * pattern[:, None, :]
    return (noise_part + aligned).reshape(ROWS).astype(jnp.float32)


def levels(stream_key, shape, cuts, least, high):
    loudness, own = 1.0, jax.random.fold_in(stream_key, 6)
    for axis_at, parts in cuts:
        heights = jnp.exp(jax.random.uniform(jax.random.fold_in(own, axis_at), (parts,), jnp.float32, least / len(cuts), high / len(cuts)))
        loudness = loudness * jnp.repeat(heights, shape[axis_at] // parts).reshape([-1 if axis == axis_at else 1 for axis in range(len(shape))])
    return loudness


def bell_draw(own_key, shape, scale, bound, shards=(), kind=jnp.bfloat16):
    values = scale * jax.random.normal(own_key, shape, jnp.float32)
    if shards:
        values = values * levels(own_key, shape, shards, -0.22, 0.18)
    return jnp.clip(values, -bound, bound).astype(kind)


def setup_inputs(seed: int = 0) -> dict:
    splits = jax.random.split(jax.random.key(seed), 7)
    return {
        "blocks": draw_blocks(jax.random.fold_in(splits[6], 71), 0),
        "block_rows": draw_block_rows(jax.random.fold_in(splits[6], 71), 0),
        "block_cols": draw_block_cols(jax.random.fold_in(splits[6], 71), 0),
        "sketch": bell_draw(splits[3], (ROWS, SKETCH), 1.0, 6.0, ((0, 2),)),
        "theta": jnp.clip(jnp.exp(math.log(10.0) - 4.6051702 * jax.random.uniform(splits[4], (COLUMNS,), jnp.float32) ** levels(splits[4], (COLUMNS,), ((0, 16),), -0.2, 0.2)), 0.1, 10.0),
        "rhs": draw_rhs(jax.random.fold_in(splits[6], 71), 0),
    }


precond_shift = 1.0
regularize = 0.5

def tile_transpose(values, rows_idx, cols_idx, inputs):
    stacked = inputs.reshape(ROW_BLOCKS, BLOCK, -1)
    picked = stacked[rows_idx]
    product = jnp.einsum('cnab,cnak->cnbk', values.astype(jnp.float32), picked, precision=lax.Precision.HIGHEST)
    onehot = (cols_idx[..., None] == jnp.arange(COL_BLOCKS, dtype=jnp.int32)).astype(jnp.float32)
    return jnp.einsum('cnj,cnbk->cjbk', onehot, product, precision=lax.Precision.HIGHEST).reshape(COLUMNS, -1)

def apply_transpose(blocks, block_rows, block_cols, inputs):
    width = inputs.shape[1]
    split_rows = inputs.reshape(GRID_ROWS, ROW_BLOCKS * BLOCK, width)

    def step(total, items):
        values, rows_idx, cols_idx, part_in = items
        return (total + tile_transpose(values, rows_idx, cols_idx, part_in), None)
    total, unused = lax.scan(step, jnp.zeros((COLUMNS, width), jnp.float32), (blocks, block_rows, block_cols, split_rows))
    return total

def apply_forward(blocks, block_rows, block_cols, inputs):
    width = inputs.shape[1]
    split_cols = inputs.reshape(GRID_COLS, COL_BLOCKS, BLOCK, width)

    def one(items):
        values, rows_idx, cols_idx = items
        picked = jax.vmap(lambda whole, index: whole[index])(split_cols, cols_idx)
        product = jnp.einsum('cnab,cnbk->cnak', values.astype(jnp.float32), picked, precision=lax.Precision.HIGHEST)
        onehot = (rows_idx[..., None] == jnp.arange(ROW_BLOCKS, dtype=jnp.int32)).astype(jnp.float32)
        return jnp.einsum('cni,cnak->iak', onehot, product, precision=lax.Precision.HIGHEST).reshape(ROW_BLOCKS * BLOCK, width)
    return lax.map(one, (blocks, block_rows, block_cols)).reshape(ROWS, width)

def solve_gram(factor, vector):
    middle = lax.linalg.triangular_solve(factor, vector[:, None], left_side=True, lower=True)
    result = lax.linalg.triangular_solve(factor, middle, left_side=True, lower=True, transpose_a=True)
    return result[:, 0]

def precondition(ysketch, factor, vector):
    coeffs = solve_gram(factor, jnp.dot(vector, ysketch, precision=lax.Precision.HIGHEST))
    return (vector - jnp.dot(ysketch, coeffs, precision=lax.Precision.HIGHEST)) / precond_shift

def reference(blocks, block_rows, block_cols, sketch, theta, rhs):
    sketch_f = sketch.astype(jnp.float32)
    sketch_cols = apply_transpose(blocks, block_rows, block_cols, sketch_f)
    scaled = (theta[:, None] * sketch_cols).astype(jnp.bfloat16)
    ysketch = apply_forward(blocks, block_rows, block_cols, scaled.astype(jnp.float32)) + regularize * sketch_f
    cross = jnp.dot(sketch_f.T, ysketch, precision=lax.Precision.HIGHEST)
    gram = precond_shift * 0.5 * (cross + cross.T) + jnp.dot(ysketch.T, ysketch, precision=lax.Precision.HIGHEST)
    factor = jnp.linalg.cholesky(gram)
    direction = precondition(ysketch, factor, rhs)
    dir_low = direction.astype(jnp.bfloat16)
    image_cols = apply_transpose(blocks, block_rows, block_cols, dir_low.astype(jnp.float32)[:, None])[:, 0]
    image_scaled = (theta * image_cols).astype(jnp.bfloat16)
    image = apply_forward(blocks, block_rows, block_cols, image_scaled.astype(jnp.float32)[:, None])[:, 0] + regularize * direction
    alpha = jnp.sum(rhs * direction) / jnp.sum(direction * image)
    solution = alpha * direction
    residual = rhs - alpha * image
    precond_residual = precondition(ysketch, factor, residual)
    return (solution, residual, precond_residual)
```

```python
import functools

import jax
import jax.numpy as jnp
from jax import lax
from jax.experimental import pallas as pl
from jax.experimental.pallas import tpu as pltpu
from jax.sharding import PartitionSpec as P

precond_shift = 1.0
regularize = 0.5
MESH = pl.DeviceIdType.MESH
HIGHEST = lax.Precision.HIGHEST
PLANE = 4
LANES = 128


def dot_nt(left, right, precision=None):
    return lax.dot_general(
        left, right, (((1,), (1,)), ((), ())), precision=precision, preferred_element_type=jnp.float32
    )


def spread(source, index, place, copies, height):
    picked = source[index]
    width, lanes = picked.shape
    if width == 1:
        tall = jnp.broadcast_to(picked, (height, lanes))
    else:
        tall = jnp.concatenate([picked] * copies, axis=0)
    group = lax.broadcasted_iota(jnp.int32, (height, lanes), 0) // width
    return jnp.where(group == place, tall, 0.0).astype(jnp.bfloat16)


def eliminate(matrix, right):
    order = matrix.shape[0]
    matrix = jnp.concatenate([matrix, jnp.zeros((order, LANES - order), jnp.float32)], axis=1)
    at = lax.broadcasted_iota(jnp.int32, (order, LANES), 0)
    for k in range(order):
        inverse = 1.0 / matrix[k : k + 1, k : k + 1]
        column = jnp.broadcast_to(matrix[:, k : k + 1], (order, LANES))
        row_m = matrix[k : k + 1, :] * inverse
        row_r = right[k : k + 1, :] * inverse
        matrix = jnp.where(at == k, row_m, matrix - column * row_m)
        right = jnp.where(at == k, row_r, right - column * row_r)
    return right


def kernel(
    cols,
    row_blocks,
    col_blocks,
    brow_ref,
    bcol_ref,
    blocks_ref,
    sketch_ref,
    theta_ref,
    rhs_ref,
    sol_ref,
    res_ref,
    pre_ref,
    vals,
    sk_t,
    s_src,
    s_dst,
    zs,
    y_src,
    y_dst,
    g_plane,
    g_depth,
    d_all,
    xs,
    e_src,
    e_dst,
    zv,
    f_src,
    f_dst,
    h_plane,
    h_depth,
    block_sem,
    pair_sem,
    y_sem,
    g_sem,
    d_sem,
    f_sem,
    h_sem,
):
    me_r = lax.axis_index("row")
    me_c = lax.axis_index("col")
    stored, order = vals.shape[0], vals.shape[1]
    width = sketch_ref.shape[1]
    pieces = order // LANES
    depth = cols // PLANE
    z, q = me_c // PLANE, me_c % PLANE
    plane = 2 * PLANE
    me_p = me_r * PLANE + q
    pending = []

    loads = []
    for n in range(stored):
        load = pltpu.make_async_copy(blocks_ref.at[n], vals.at[n], block_sem.at[n])
        load.start()
        loads.append(load)

    barrier = pltpu.get_barrier_semaphore()
    for t in range(1, cols):
        pl.semaphore_signal(
            barrier, inc=1, device_id=(me_r, lax.rem(me_c + t, cols)), device_id_type=MESH
        )
    for u in range(PLANE):
        pl.semaphore_signal(
            barrier, inc=1, device_id=(1 - me_r, z * PLANE + u), device_id_type=MESH
        )

    def send(src, dst, sems, at, device):
        copy = pltpu.make_async_remote_copy(
            src_ref=src,
            dst_ref=dst,
            send_sem=sems.at[0, at],
            recv_sem=sems.at[1, at],
            device_id=device,
            device_id_type=MESH,
        )
        copy.start()
        pending.append(copy)
        return copy

    def all_reduce(value, first, second, sems):
        first[me_p] = value
        copies = []
        for u in range(1, plane):
            peer = lax.rem(me_p + u, plane)
            device = (peer // PLANE, z * PLANE + lax.rem(peer, PLANE))
            copies.append(send(first.at[me_p], first.at[me_p], sems, u - 1, device))
        for copy in copies:
            copy.wait_recv()
        total = first[0]
        for u in range(1, plane):
            total = total + first[u]
        second[z] = total
        copies = []
        for u in range(1, depth):
            device = (me_r, lax.rem(z + u, depth) * PLANE + q)
            copies.append(send(second.at[z], second.at[z], sems, plane - 2 + u, device))
        for copy in copies:
            copy.wait_recv()
        total = second[0]
        for u in range(1, depth):
            total = total + second[u]
        return total

    def scatter_sum(src, dst, sems):
        copies = []
        for t in range(1, cols):
            to = lax.rem(me_c + t, cols)
            copies.append(send(src.at[to], dst.at[t], sems, t, (me_r, to)))
        total = src[me_c]
        for t, copy in enumerate(copies, 1):
            copy.wait_recv()
            total = total + dst[t]
        return total

    def strip(ref, j):
        return jnp.concatenate([ref[pieces * j + p : pieces * j + p + 1, :] for p in range(pieces)], axis=1)

    eye = (
        lax.broadcasted_iota(jnp.int32, (width, width), 0)
        == lax.broadcasted_iota(jnp.int32, (width, width), 1)
    )
    eye = jnp.where(eye, 1.0, 0.0).astype(jnp.bfloat16)
    for i in range(row_blocks):
        sk_t[i] = dot_nt(eye, sketch_ref[i * order : (i + 1) * order, :])
    omega = dot_nt(eye, sketch_ref[pl.ds(pl.multiple_of(me_c * LANES, LANES), LANES), :])
    rhs = jnp.broadcast_to(rhs_ref[pl.ds(me_c, 1), :], (8, LANES))

    total = jnp.zeros((col_blocks * width, order), jnp.float32)
    for n in range(stored):
        left = spread(sk_t, brow_ref[n], bcol_ref[n], col_blocks, col_blocks * width)
        loads[n].wait()
        total = total + jnp.dot(left, vals[n], preferred_element_type=jnp.float32)
    s_src[...] = total
    pl.semaphore_wait(barrier, cols - 1 + PLANE)
    send(s_src, s_dst, pair_sem, 0, (1 - me_r, me_c)).wait_recv()
    for j in range(col_blocks):
        part = slice(j * width, (j + 1) * width)
        scaled = (strip(theta_ref, j) * (s_src[part, :] + s_dst[part, :])).astype(jnp.bfloat16)
        zs[j] = scaled.astype(jnp.float32)

    total = jnp.zeros((row_blocks * width, order), jnp.float32)
    for n in range(stored):
        left = spread(zs, bcol_ref[n], brow_ref[n], row_blocks, row_blocks * width)
        total = total + dot_nt(left, vals[n])
    for i in range(row_blocks):
        for p in range(pieces):
            y_src[pieces * i + p] = total[i * width : (i + 1) * width, p * LANES : (p + 1) * LANES]
    y_t = scatter_sum(y_src, y_dst, y_sem) + regularize * omega

    both = y_t + precond_shift * omega
    first = dot_nt(jnp.concatenate([both, rhs], axis=0), y_t, HIGHEST)
    gram = 0.5 * (first[:width] + dot_nt(y_t, both, HIGHEST))
    packs = LANES // width
    tall = width // packs
    packed = jnp.concatenate([gram[s * tall : (s + 1) * tall] for s in range(packs)], axis=1)
    sketched = jnp.concatenate([first[width:]] * packs, axis=1)
    summed = all_reduce(jnp.concatenate([packed, sketched], axis=0), g_plane, g_depth, g_sem)
    gram = jnp.concatenate([summed[:tall, s * width : (s + 1) * width] for s in range(packs)], axis=0)
    sketched_rhs = summed[tall:, :width]
    weights = eliminate(gram, y_t)
    direction = (rhs - jnp.dot(sketched_rhs, weights, precision=HIGHEST)) / precond_shift

    d_all[me_c] = direction[:1]
    copies = [
        send(d_all.at[me_c], d_all.at[me_c], d_sem, t, (me_r, lax.rem(me_c + t, cols)))
        for t in range(1, cols)
    ]
    for copy in copies:
        copy.wait_recv()
    for i in range(row_blocks):
        line = jnp.concatenate([d_all[pieces * i + p] for p in range(pieces)], axis=1)
        xs[i] = line.astype(jnp.bfloat16).astype(jnp.float32)
    total = jnp.zeros((16, order), jnp.float32)
    for n in range(stored):
        left = spread(xs, brow_ref[n], bcol_ref[n], col_blocks, 16)
        total = total + jnp.dot(left, vals[n], preferred_element_type=jnp.float32)
    e_src[...] = total[:8]
    send(e_src, e_dst, pair_sem, 1, (1 - me_r, me_c)).wait_recv()
    image_cols = e_src[...] + e_dst[...]
    for j in range(col_blocks):
        line = (strip(theta_ref, j) * image_cols[j : j + 1]).astype(jnp.bfloat16)
        zv[j] = line.astype(jnp.float32)
    total = jnp.zeros((16, order), jnp.float32)
    for n in range(stored):
        left = spread(zv, bcol_ref[n], brow_ref[n], row_blocks, 16)
        total = total + dot_nt(left, vals[n])
    for i in range(row_blocks):
        for p in range(pieces):
            f_src[pieces * i + p] = total[i : i + 1, p * LANES : (p + 1) * LANES]
    image = jnp.broadcast_to(scatter_sum(f_src, f_dst, f_sem), (8, LANES)) + regularize * direction

    against = dot_nt(image, y_t, HIGHEST)
    curvature = jnp.sum(direction * image, axis=1, keepdims=True)
    along = jnp.sum(rhs * direction, axis=1, keepdims=True)
    against = jnp.concatenate([against, jnp.zeros((8, LANES - width), jnp.float32)], axis=1)
    lane = lax.broadcasted_iota(jnp.int32, (8, LANES), 1)
    value = jnp.where(lane == width, curvature, jnp.where(lane == width + 1, along, against))
    summed = all_reduce(value, h_plane, h_depth, h_sem)
    alpha = summed[:, width + 1 : width + 2] / summed[:, width : width + 1]
    residual = rhs - alpha * image
    sketched_res = sketched_rhs - alpha * summed[:, :width]
    pre = (residual - jnp.dot(sketched_res, weights, precision=HIGHEST)) / precond_shift
    sol_ref[...] = (alpha * direction)[:1]
    res_ref[...] = residual[:1]
    pre_ref[...] = pre[:1]
    for copy in pending:
        copy.wait_send()


def fused(cols, blocks, block_rows, block_cols, sketch, theta, rhs):
    stored, order = blocks.shape[2], blocks.shape[3]
    width = sketch.shape[1]
    row_blocks = sketch.shape[0] // order
    col_blocks = theta.shape[0] // order
    depth = cols // PLANE
    vmem = pl.BlockSpec(memory_space=pltpu.VMEM)
    smem = pl.BlockSpec(memory_space=pltpu.SMEM)
    line = jax.ShapeDtypeStruct((1, LANES), jnp.float32)
    f32 = jnp.float32
    outs = pl.pallas_call(
        functools.partial(kernel, cols, row_blocks, col_blocks),
        out_shape=(line, line, line),
        in_specs=[smem, smem, pl.BlockSpec(memory_space=pl.ANY), vmem, vmem, vmem],
        out_specs=(vmem, vmem, vmem),
        scratch_shapes=[
            pltpu.VMEM((stored, order, order), jnp.bfloat16),
            pltpu.VMEM((row_blocks, width, order), f32),
            pltpu.VMEM((col_blocks * width, order), f32),
            pltpu.VMEM((col_blocks * width, order), f32),
            pltpu.VMEM((col_blocks, width, order), f32),
            pltpu.VMEM((cols, width, LANES), f32),
            pltpu.VMEM((cols, width, LANES), f32),
            pltpu.VMEM((2 * PLANE, 16, LANES), f32),
            pltpu.VMEM((depth, 16, LANES), f32),
            pltpu.VMEM((cols, 1, LANES), f32),
            pltpu.VMEM((row_blocks, 1, order), f32),
            pltpu.VMEM((8, order), f32),
            pltpu.VMEM((8, order), f32),
            pltpu.VMEM((col_blocks, 1, order), f32),
            pltpu.VMEM((cols, 1, LANES), f32),
            pltpu.VMEM((cols, 1, LANES), f32),
            pltpu.VMEM((2 * PLANE, 8, LANES), f32),
            pltpu.VMEM((depth, 8, LANES), f32),
            pltpu.SemaphoreType.DMA((stored,)),
            pltpu.SemaphoreType.DMA((2, 2)),
            pltpu.SemaphoreType.DMA((2, cols)),
            pltpu.SemaphoreType.DMA((2, 2 * PLANE + depth)),
            pltpu.SemaphoreType.DMA((2, cols)),
            pltpu.SemaphoreType.DMA((2, cols)),
            pltpu.SemaphoreType.DMA((2, 2 * PLANE + depth)),
        ],
        compiler_params=pltpu.CompilerParams(
            collective_id=0, has_side_effects=True, vmem_limit_bytes=32 * 1024 * 1024
        ),
    )(
        block_rows.reshape(stored),
        block_cols.reshape(stored),
        blocks.reshape(stored, order, order),
        sketch,
        theta.reshape(-1, LANES),
        rhs.reshape(-1, LANES),
    )
    return tuple(out.reshape(LANES) for out in outs)


def tile_transpose(values, rows_idx, cols_idx, inputs, col_count):
    order = values.shape[1]
    width = inputs.shape[1]
    picked = inputs.reshape(-1, order, width)[rows_idx]
    product = jnp.einsum("nab,nak->nbk", values, picked, preferred_element_type=jnp.float32)
    onehot = (cols_idx[:, None] == jnp.arange(col_count, dtype=jnp.int32)[None, :]).astype(
        jnp.float32
    )
    merged = jnp.einsum("nj,nbk->jbk", onehot, product, precision=lax.Precision.HIGHEST)
    return merged.reshape(col_count * order, width)


def tile_forward(values, rows_idx, cols_idx, inputs, row_count):
    order = values.shape[1]
    width = inputs.shape[1]
    picked = inputs.reshape(-1, order, width)[cols_idx]
    product = jnp.einsum("nab,nbk->nak", values, picked, preferred_element_type=jnp.float32)
    onehot = (rows_idx[:, None] == jnp.arange(row_count, dtype=jnp.int32)[None, :]).astype(
        jnp.float32
    )
    merged = jnp.einsum("ni,nak->iak", onehot, product, precision=lax.Precision.HIGHEST)
    return merged.reshape(row_count * order, width)


def solve_gram(factor, vector):
    middle = lax.linalg.triangular_solve(factor, vector[:, None], left_side=True, lower=True)
    result = lax.linalg.triangular_solve(
        factor, middle, left_side=True, lower=True, transpose_a=True
    )
    return result[:, 0]


def shards(blocks, block_rows, block_cols, sketch, theta, rhs):
    values = blocks[0, 0]
    rows_idx = block_rows[0, 0]
    cols_idx = block_cols[0, 0]
    order = values.shape[1]
    local_rows = sketch.shape[0]
    row_count = local_rows // order
    col_count = theta.shape[0] // order
    share = local_rows // lax.axis_size("col")
    offset = lax.axis_index("col") * share
    sketch_f = sketch.astype(jnp.float32)
    sketch_part = lax.dynamic_slice_in_dim(sketch_f, offset, share, 0)
    rhs_part = lax.dynamic_slice_in_dim(rhs, offset, share, 0)
    col_terms = tile_transpose(values, rows_idx, cols_idx, sketch, col_count)
    sketch_cols = lax.psum(col_terms, "row")
    scaled = (theta[:, None] * sketch_cols).astype(jnp.bfloat16)
    row_terms = tile_forward(values, rows_idx, cols_idx, scaled, row_count)
    ysketch = lax.psum(row_terms, "col") + regularize * sketch_f
    y_part = lax.dynamic_slice_in_dim(ysketch, offset, share, 0)
    cross = jnp.dot(sketch_part.T, y_part, precision=lax.Precision.HIGHEST)
    gram_terms = precond_shift * 0.5 * (cross + cross.T) + jnp.dot(
        y_part.T, y_part, precision=lax.Precision.HIGHEST
    )
    yb_terms = jnp.dot(rhs_part, y_part, precision=lax.Precision.HIGHEST)
    gram, sketched_rhs = lax.psum((gram_terms, yb_terms), ("row", "col"))
    factor = jnp.linalg.cholesky(gram)
    coeffs = solve_gram(factor, sketched_rhs)
    direction_full = (
        rhs - jnp.dot(ysketch, coeffs, precision=lax.Precision.HIGHEST)
    ) / precond_shift
    direction = lax.dynamic_slice_in_dim(direction_full, offset, share, 0)
    dir_low = direction_full.astype(jnp.bfloat16)
    image_terms = tile_transpose(values, rows_idx, cols_idx, dir_low[:, None], col_count)[:, 0]
    image_cols = lax.psum(image_terms, "row")
    image_scaled = (theta * image_cols).astype(jnp.bfloat16)
    product_terms = tile_forward(values, rows_idx, cols_idx, image_scaled[:, None], row_count)[:, 0]
    image_full = lax.psum(product_terms, "col")
    image = lax.dynamic_slice_in_dim(image_full, offset, share, 0) + regularize * direction
    along = lax.psum(jnp.sum(rhs_part * direction), ("row", "col"))
    curvature = lax.psum(jnp.sum(direction * image), ("row", "col"))
    alpha = along / curvature
    residual = rhs_part - alpha * image
    sketched_res = lax.psum(
        jnp.dot(residual, y_part, precision=lax.Precision.HIGHEST), ("row", "col")
    )
    solution = alpha * direction
    res_coeffs = solve_gram(factor, sketched_res)
    precond_residual = (
        residual - jnp.dot(y_part, res_coeffs, precision=lax.Precision.HIGHEST)
    ) / precond_shift
    return (solution, residual, precond_residual)


def solution(mesh):
    in_specs = (
        P("row", "col", None, None, None),
        P("row", "col", None),
        P("row", "col", None),
        P("row", None),
        P("col"),
        P("row"),
    )
    out_specs = (P(("row", "col")), P(("row", "col")), P(("row", "col")))
    cols = mesh.shape["col"]

    def step(blocks, block_rows, block_cols, sketch, theta, rhs):
        share = sketch.shape[0] // cols
        if mesh.shape["row"] == 2 and cols % PLANE == 0 and share == LANES:
            return fused(cols, blocks, block_rows, block_cols, sketch, theta, rhs)
        return shards(blocks, block_rows, block_cols, sketch, theta, rhs)

    return jax.shard_map(step, mesh=mesh, in_specs=in_specs, out_specs=out_specs, check_vma=False)
```

```python
import functools

import jax
import jax.numpy as jnp
from jax import lax
from jax.experimental import pallas as pl
from jax.experimental.pallas import tpu as pltpu
from jax.sharding import PartitionSpec as P

precond_shift = 1.0
regularize = 0.5
MESH = pl.DeviceIdType.MESH
HIGHEST = lax.Precision.HIGHEST
PLANE = 4
LANES = 128
VMEM_BYTES = 64 * 1024 * 1024


def dot_nt(left, right, precision=None):
    return lax.dot_general(
        left, right, (((1,), (1,)), ((), ())), precision=precision, preferred_element_type=jnp.float32
    )


def spread(source, index, place, copies, height):
    picked = source[index]
    width, lanes = picked.shape
    if width == 1:
        tall = jnp.broadcast_to(picked, (height, lanes))
    else:
        tall = jnp.concatenate([picked] * copies, axis=0)
    group = lax.broadcasted_iota(jnp.int32, (height, lanes), 0) // width
    return jnp.where(group == place, tall, 0.0).astype(jnp.bfloat16)


def eliminate(matrix):
    order = matrix.shape[0]
    panel = 8
    at = lax.broadcasted_iota(jnp.int32, (order, LANES), 0)
    lane = lax.broadcasted_iota(jnp.int32, (order, LANES), 1)
    rest = LANES - matrix.shape[1]
    wide = jnp.concatenate([matrix, jnp.zeros((order, rest), jnp.float32)], axis=1)
    wide = jnp.where(lane == at + 2 * order, 1.0, wide)
    for start in range(0, order, panel):
        columns = [
            jnp.broadcast_to(wide[:, k : k + 1], (order, LANES)) for k in range(start, start + panel)
        ]
        for j in range(panel):
            k = start + j
            here = at == k
            column = columns[j]
            inverse = 1.0 / column[k : k + 1]
            for other in range(j + 1, panel):
                row = columns[other][k : k + 1] * inverse
                columns[other] = jnp.where(here, row, columns[other] - column * row)
            row = wide[k : k + 1] * inverse
            wide = jnp.where(here, row, wide - column * row)
    return wide[:, order : order + 1], wide[:, 2 * order : 3 * order]


def kernel(
    cols,
    row_blocks,
    col_blocks,
    brow_hbm,
    bcol_hbm,
    blocks_ref,
    sketch_hbm,
    theta_hbm,
    rhs_hbm,
    out_ref,
    brow_ref,
    bcol_ref,
    sketch_ref,
    theta_ref,
    rhs_ref,
    vals,
    sk_t,
    s_src,
    s_dst,
    zs,
    y_own,
    y_pair,
    y_src,
    y_dst,
    y_all,
    g_plane,
    g_depth,
    xs,
    e_src,
    e_dst,
    zv,
    f_src,
    f_dst,
    h_plane,
    h_depth,
    load_sem,
    pair_sem,
    y_sem,
    a_sem,
    g_sem,
    f_sem,
    h_sem,
):
    me_r = lax.axis_index("row")
    me_c = lax.axis_index("col")
    stored, order = vals.shape[0], vals.shape[1]
    width = sketch_ref.shape[0]
    pieces = order // LANES
    depth = cols // PLANE
    z, q = me_c // PLANE, me_c % PLANE
    plane = 2 * PLANE
    me_p = me_r * PLANE + q
    core, chip, chips = lax.rem(me_c, 2), me_c // 2, cols // 2
    twin = (me_r, chip * 2 + 1 - core)
    pending = []

    smalls = []
    for at, (src, dst) in enumerate(
        [
            (sketch_hbm, sketch_ref),
            (brow_hbm, brow_ref),
            (bcol_hbm, bcol_ref),
            (theta_hbm, theta_ref),
            (rhs_hbm, rhs_ref),
        ]
    ):
        load = pltpu.make_async_copy(src, dst, load_sem.at[stored + at])
        load.start()
        smalls.append(load)
    loads = []
    for n in range(stored):
        load = pltpu.make_async_copy(blocks_ref.at[n], vals.at[n], load_sem.at[n])
        load.start()
        loads.append(load)

    barrier = pltpu.get_barrier_semaphore()
    for t in range(1, cols):
        pl.semaphore_signal(
            barrier, inc=1, device_id=(me_r, lax.rem(me_c + t, cols)), device_id_type=MESH
        )
    for u in range(PLANE):
        pl.semaphore_signal(
            barrier, inc=1, device_id=(1 - me_r, z * PLANE + u), device_id_type=MESH
        )

    def send(src, dst, sems, at, device):
        copy = pltpu.make_async_remote_copy(
            src_ref=src,
            dst_ref=dst,
            send_sem=sems.at[0, at],
            recv_sem=sems.at[1, at],
            device_id=device,
            device_id_type=MESH,
        )
        copy.start()
        pending.append(copy)
        return copy

    def reduce_start(value, first, sems):
        first[me_p] = value
        copies = []
        for u in range(1, plane):
            peer = lax.rem(me_p + u, plane)
            device = (peer // PLANE, z * PLANE + lax.rem(peer, PLANE))
            copies.append(send(first.at[me_p], first.at[me_p], sems, u - 1, device))
        return copies

    def reduce_middle(copies, first, second, sems):
        for copy in copies:
            copy.wait_recv()
        total = first[0]
        for u in range(1, plane):
            total = total + first[u]
        second[z] = total
        copies = []
        for u in range(1, depth):
            device = (me_r, lax.rem(z + u, depth) * PLANE + q)
            copies.append(send(second.at[z], second.at[z], sems, plane - 2 + u, device))
        return copies

    def reduce_finish(copies, second):
        for copy in copies:
            copy.wait_recv()
        total = second[0]
        for u in range(1, depth):
            total = total + second[u]
        return total

    def scatter_start(src, dst, sems):
        copies = []
        for t in range(1, cols):
            to = lax.rem(me_c + t, cols)
            copies.append(send(src.at[to], dst.at[t], sems, t, (me_r, to)))
        return copies

    def scatter_finish(total, copies, dst):
        for t, copy in enumerate(copies, 1):
            copy.wait_recv()
            total = total + dst[t]
        return total

    def strip(ref, j):
        return jnp.concatenate([ref[pieces * j + p : pieces * j + p + 1, :] for p in range(pieces)], axis=1)

    for load in smalls:
        load.wait()
    for i in range(row_blocks):
        sk_t[i] = sketch_ref[:, i * order : (i + 1) * order].astype(jnp.float32)
    own = pl.ds(pl.multiple_of(me_c * LANES, LANES), LANES)
    omega = sketch_ref[:, own].astype(jnp.float32)
    rhs = jnp.broadcast_to(rhs_ref[pl.ds(me_c, 1), :], (8, LANES))

    halves = 2
    half = order // halves
    lefts = [
        spread(sk_t, brow_ref[n], bcol_ref[n], col_blocks, col_blocks * width) for n in range(stored)
    ]
    mine, copies = [], []
    for h in range(halves):
        part = slice(h * half, (h + 1) * half)
        total = jnp.zeros((col_blocks * width, half), jnp.float32)
        for n in range(stored):
            if h == 0:
                loads[n].wait()
            total = total + jnp.dot(lefts[n], vals[n, :, part], preferred_element_type=jnp.float32)
        s_src[h] = total.astype(jnp.bfloat16)
        mine.append(total)
        if h == 0:
            pl.semaphore_wait(barrier, cols - 1 + PLANE)
        copies.append(send(s_src.at[h], s_dst.at[h], pair_sem, h, (1 - me_r, me_c)))
    total = jnp.zeros((row_blocks * width, order), jnp.float32)
    for h in range(halves):
        part = slice(h * half, (h + 1) * half)
        copies[h].wait_recv()
        summed = mine[h] + s_dst[h].astype(jnp.float32)
        for j in range(col_blocks):
            scaled = strip(theta_ref, j)[:, part] * summed[j * width : (j + 1) * width]
            zs[h, j] = scaled.astype(jnp.bfloat16).astype(jnp.float32)
        for n in range(stored):
            left = spread(zs.at[h], bcol_ref[n], brow_ref[n], row_blocks, row_blocks * width)
            total = total + dot_nt(left, vals[n, :, part])
    for i in range(row_blocks):
        for p in range(pieces):
            at = pieces * i + p
            y_own[at % 2, at // 2] = total[i * width : (i + 1) * width, p * LANES : (p + 1) * LANES]
    copy = send(y_own.at[1 - core], y_pair, pair_sem, halves, twin)
    copy.wait_recv()
    for t in range(chips):
        y_src[t] = y_own[core, t] + y_pair[t]
    copies = []
    for t in range(1, chips):
        to = lax.rem(chip + t, chips)
        copies.append(send(y_src.at[to], y_dst.at[t], y_sem, t, (me_r, to * 2 + core)))
    y_t = scatter_finish(y_src[chip] + regularize * omega, copies, y_dst)
    y_all[core, chip] = y_t

    both = y_t + precond_shift * omega
    tall_rhs = jnp.broadcast_to(rhs[:1], (width, LANES))
    upper = jnp.concatenate([0.5 * y_t, 0.5 * both], axis=1)
    lower = jnp.concatenate([jnp.zeros((width, LANES), jnp.float32), tall_rhs], axis=1)
    joined = dot_nt(
        jnp.concatenate([both, y_t], axis=1), jnp.concatenate([upper, lower], axis=0), HIGHEST
    )
    packs = LANES // (2 * width)
    tall = width // packs
    packed = jnp.concatenate([joined[s * tall : (s + 1) * tall] for s in range(packs)], axis=1)
    copies = reduce_start(packed, g_plane, g_sem)
    gathers = []
    for t in range(1, chips):
        to = lax.rem(chip + t, chips)
        gathers.append(send(y_all.at[core, chip], y_all.at[core, chip], a_sem, t, (me_r, to * 2 + core)))
    copies = reduce_middle(copies, g_plane, g_depth, g_sem)
    for copy in gathers:
        copy.wait_recv()
    gathered = send(y_all.at[core], y_all.at[core], a_sem, 0, twin)
    summed = reduce_finish(copies, g_depth)
    joined = jnp.concatenate(
        [summed[:, s * 2 * width : (s + 1) * 2 * width] for s in range(packs)], axis=0
    )
    sketched_rhs = joined[:, width : width + 1]
    coeffs, inverse = eliminate(joined)
    coeffs = jnp.broadcast_to(coeffs, (width, LANES))
    taken = jnp.sum(coeffs * y_t, axis=0, keepdims=True)
    direction = (rhs[:1] - taken) / precond_shift

    gathered.wait_recv()
    lines = []
    for i in range(row_blocks):
        taken = []
        for p in range(pieces):
            at = pieces * i + p
            taken.append(jnp.sum(coeffs * y_all[at % 2, at // 2], axis=0, keepdims=True))
        line = (strip(rhs_ref, i) - jnp.concatenate(taken, axis=1)) / precond_shift
        lines.append(line)
        xs[i] = line.astype(jnp.bfloat16).astype(jnp.float32)
    total = jnp.zeros((16, order), jnp.float32)
    for n in range(stored):
        left = spread(xs, brow_ref[n], bcol_ref[n], col_blocks, 16)
        total = total + jnp.dot(left, vals[n], preferred_element_type=jnp.float32)
    e_src[...] = total[:8]
    copy = send(e_src, e_dst, pair_sem, halves + 1, (1 - me_r, me_c))
    weights = jnp.dot(inverse, y_t, precision=HIGHEST)
    copy.wait_recv()
    image_cols = e_src[...] + e_dst[...]
    for j in range(col_blocks):
        line = (strip(theta_ref, j) * image_cols[j : j + 1]).astype(jnp.bfloat16)
        zv[j] = line.astype(jnp.float32)
    total = jnp.zeros((16, order), jnp.float32)
    for n in range(stored):
        left = spread(zv, bcol_ref[n], brow_ref[n], row_blocks, 16)
        total = total + dot_nt(left, vals[n])

    against = regularize * y_t * direction
    curvature = regularize * direction * direction
    for i in range(row_blocks):
        for p in range(pieces):
            part = slice(p * LANES, (p + 1) * LANES)
            piece = total[i : i + 1, part]
            f_src[pieces * i + p] = piece
            against = against + y_all[(pieces * i + p) % 2, (pieces * i + p) // 2] * piece
            curvature = curvature + lines[i][:, part] * piece
    at = lax.broadcasted_iota(jnp.int32, (width, LANES), 0)
    diagonal = lax.broadcasted_iota(jnp.int32, (width, LANES), 1) == at
    against = jnp.where(diagonal, jnp.sum(against, axis=1, keepdims=True), 0.0)
    against = jnp.sum(against, axis=0, keepdims=True)
    curvature = jnp.sum(curvature, axis=1, keepdims=True)
    along = jnp.sum(rhs[:1] * direction, axis=1, keepdims=True)
    lane = lax.broadcasted_iota(jnp.int32, (1, LANES), 1)
    value = jnp.where(lane == width, curvature, jnp.where(lane == width + 1, along, against))
    copies = reduce_start(value, h_plane, h_sem)
    scatters = scatter_start(f_src, f_dst, f_sem)
    copies = reduce_middle(copies, h_plane, h_depth, h_sem)
    image = scatter_finish(f_src[me_c], scatters, f_dst)
    summed = reduce_finish(copies, h_depth)
    alpha = summed[:, width + 1 : width + 2] / summed[:, width : width + 1]
    sketched = jnp.sum(jnp.where(diagonal, summed, 0.0), axis=1, keepdims=True)
    taken = jnp.sum((sketched_rhs - alpha * sketched) * weights, axis=0, keepdims=True)
    out_ref[0:1] = jnp.broadcast_to(alpha, (1, LANES))
    out_ref[1:2] = direction
    out_ref[2:3] = rhs[:1]
    out_ref[3:4] = image
    out_ref[4:5] = taken
    out_ref[5:8] = jnp.zeros((3, LANES), jnp.float32)
    for copy in pending:
        copy.wait_send()


def fused(cols, blocks, block_rows, block_cols, sketch, theta, rhs):
    stored, order = blocks.shape[2], blocks.shape[3]
    local, width = sketch.shape
    row_blocks = local // order
    col_blocks = theta.shape[0] // order
    depth = cols // PLANE
    vmem = pl.BlockSpec(memory_space=pltpu.VMEM)
    hbm = pl.BlockSpec(memory_space=pl.ANY)
    f32, bf16 = jnp.float32, jnp.bfloat16
    reduce_sems = pltpu.SemaphoreType.DMA((2, 2 * PLANE + depth))
    col_sems = pltpu.SemaphoreType.DMA((2, cols))
    out = pl.pallas_call(
        functools.partial(kernel, cols, row_blocks, col_blocks),
        out_shape=jax.ShapeDtypeStruct((8, LANES), jnp.float32),
        in_specs=[hbm] * 6,
        out_specs=vmem,
        scratch_shapes=[
            pltpu.SMEM((stored,), jnp.int32),
            pltpu.SMEM((stored,), jnp.int32),
            pltpu.VMEM((width, local), bf16),
            pltpu.VMEM((theta.shape[0] // LANES, LANES), f32),
            pltpu.VMEM((local // LANES, LANES), f32),
            pltpu.VMEM((stored, order, order), bf16),
            pltpu.VMEM((row_blocks, width, order), f32),
            pltpu.VMEM((2, col_blocks * width, order // 2), bf16),
            pltpu.VMEM((2, col_blocks * width, order // 2), bf16),
            pltpu.VMEM((2, col_blocks, width, order // 2), f32),
            pltpu.VMEM((2, cols // 2, width, LANES), f32),
            pltpu.VMEM((cols // 2, width, LANES), f32),
            pltpu.VMEM((cols // 2, width, LANES), f32),
            pltpu.VMEM((cols // 2, width, LANES), f32),
            pltpu.VMEM((2, cols // 2, width, LANES), f32),
            pltpu.VMEM((2 * PLANE, 16, LANES), f32),
            pltpu.VMEM((depth, 16, LANES), f32),
            pltpu.VMEM((row_blocks, 1, order), f32),
            pltpu.VMEM((8, order), f32),
            pltpu.VMEM((8, order), f32),
            pltpu.VMEM((col_blocks, 1, order), f32),
            pltpu.VMEM((cols, 1, LANES), f32),
            pltpu.VMEM((cols, 1, LANES), f32),
            pltpu.VMEM((2 * PLANE, 1, LANES), f32),
            pltpu.VMEM((depth, 1, LANES), f32),
            pltpu.SemaphoreType.DMA((stored + 5,)),
            pltpu.SemaphoreType.DMA((2, 4)),
            col_sems,
            col_sems,
            reduce_sems,
            col_sems,
            reduce_sems,
        ],
        compiler_params=pltpu.CompilerParams(
            collective_id=0, has_side_effects=True, vmem_limit_bytes=VMEM_BYTES
        ),
    )(
        block_rows.reshape(stored),
        block_cols.reshape(stored),
        blocks.reshape(stored, order, order),
        sketch.T,
        theta.reshape(-1, LANES),
        rhs.reshape(-1, LANES),
    )
    alpha, direction, mine, image, taken = (out[i] for i in range(5))
    iterate = alpha * direction
    residual = mine - alpha * image - regularize * iterate
    return iterate, residual, (residual - taken) / precond_shift


def tile_transpose(values, rows_idx, cols_idx, inputs, col_count):
    order = values.shape[1]
    width = inputs.shape[1]
    picked = inputs.reshape(-1, order, width)[rows_idx]
    product = jnp.einsum("nab,nak->nbk", values, picked, preferred_element_type=jnp.float32)
    onehot = (cols_idx[:, None] == jnp.arange(col_count, dtype=jnp.int32)[None, :]).astype(
        jnp.float32
    )
    merged = jnp.einsum("nj,nbk->jbk", onehot, product, precision=lax.Precision.HIGHEST)
    return merged.reshape(col_count * order, width)


def tile_forward(values, rows_idx, cols_idx, inputs, row_count):
    order = values.shape[1]
    width = inputs.shape[1]
    picked = inputs.reshape(-1, order, width)[cols_idx]
    product = jnp.einsum("nab,nbk->nak", values, picked, preferred_element_type=jnp.float32)
    onehot = (rows_idx[:, None] == jnp.arange(row_count, dtype=jnp.int32)[None, :]).astype(
        jnp.float32
    )
    merged = jnp.einsum("ni,nak->iak", onehot, product, precision=lax.Precision.HIGHEST)
    return merged.reshape(row_count * order, width)


def solve_gram(factor, vector):
    middle = lax.linalg.triangular_solve(factor, vector[:, None], left_side=True, lower=True)
    result = lax.linalg.triangular_solve(
        factor, middle, left_side=True, lower=True, transpose_a=True
    )
    return result[:, 0]


def shards(blocks, block_rows, block_cols, sketch, theta, rhs):
    values = blocks[0, 0]
    rows_idx = block_rows[0, 0]
    cols_idx = block_cols[0, 0]
    order = values.shape[1]
    local_rows = sketch.shape[0]
    row_count = local_rows // order
    col_count = theta.shape[0] // order
    share = local_rows // lax.axis_size("col")
    offset = lax.axis_index("col") * share
    sketch_f = sketch.astype(jnp.float32)
    sketch_part = lax.dynamic_slice_in_dim(sketch_f, offset, share, 0)
    rhs_part = lax.dynamic_slice_in_dim(rhs, offset, share, 0)
    col_terms = tile_transpose(values, rows_idx, cols_idx, sketch, col_count)
    sketch_cols = lax.psum(col_terms, "row")
    scaled = (theta[:, None] * sketch_cols).astype(jnp.bfloat16)
    row_terms = tile_forward(values, rows_idx, cols_idx, scaled, row_count)
    ysketch = lax.psum(row_terms, "col") + regularize * sketch_f
    y_part = lax.dynamic_slice_in_dim(ysketch, offset, share, 0)
    cross = jnp.dot(sketch_part.T, y_part, precision=lax.Precision.HIGHEST)
    gram_terms = precond_shift * 0.5 * (cross + cross.T) + jnp.dot(
        y_part.T, y_part, precision=lax.Precision.HIGHEST
    )
    yb_terms = jnp.dot(rhs_part, y_part, precision=lax.Precision.HIGHEST)
    gram, sketched_rhs = lax.psum((gram_terms, yb_terms), ("row", "col"))
    factor = jnp.linalg.cholesky(gram)
    coeffs = solve_gram(factor, sketched_rhs)
    direction_full = (
        rhs - jnp.dot(ysketch, coeffs, precision=lax.Precision.HIGHEST)
    ) / precond_shift
    direction = lax.dynamic_slice_in_dim(direction_full, offset, share, 0)
    dir_low = direction_full.astype(jnp.bfloat16)
    image_terms = tile_transpose(values, rows_idx, cols_idx, dir_low[:, None], col_count)[:, 0]
    image_cols = lax.psum(image_terms, "row")
    image_scaled = (theta * image_cols).astype(jnp.bfloat16)
    product_terms = tile_forward(values, rows_idx, cols_idx, image_scaled[:, None], row_count)[:, 0]
    image_full = lax.psum(product_terms, "col")
    image = lax.dynamic_slice_in_dim(image_full, offset, share, 0) + regularize * direction
    along = lax.psum(jnp.sum(rhs_part * direction), ("row", "col"))
    curvature = lax.psum(jnp.sum(direction * image), ("row", "col"))
    alpha = along / curvature
    residual = rhs_part - alpha * image
    sketched_res = lax.psum(
        jnp.dot(residual, y_part, precision=lax.Precision.HIGHEST), ("row", "col")
    )
    solution = alpha * direction
    res_coeffs = solve_gram(factor, sketched_res)
    precond_residual = (
        residual - jnp.dot(y_part, res_coeffs, precision=lax.Precision.HIGHEST)
    ) / precond_shift
    return (solution, residual, precond_residual)


def solution(mesh):
    in_specs = (
        P("row", "col", None, None, None),
        P("row", "col", None),
        P("row", "col", None),
        P("row", None),
        P("col"),
        P("row"),
    )
    out_specs = (P(("row", "col")), P(("row", "col")), P(("row", "col")))
    cols = mesh.shape["col"]

    def step(blocks, block_rows, block_cols, sketch, theta, rhs):
        share = sketch.shape[0] // cols
        if mesh.shape["row"] == 2 and cols % PLANE == 0 and share == LANES:
            return fused(cols, blocks, block_rows, block_cols, sketch, theta, rhs)
        return shards(blocks, block_rows, block_cols, sketch, theta, rhs)

    return jax.shard_map(step, mesh=mesh, in_specs=in_specs, out_specs=out_specs, check_vma=False)
```

```python
import functools

import jax
import jax.numpy as jnp
from jax import lax
from jax.experimental import pallas as pl
from jax.experimental.pallas import tpu as pltpu
from jax.sharding import PartitionSpec as P

precond_shift = 1.0
regularize = 0.5
MESH = pl.DeviceIdType.MESH
HIGHEST = lax.Precision.HIGHEST
PLANE = 4
LANES = 128
VMEM_BYTES = 64 * 1024 * 1024


def dot_nt(left, right, precision=None):
    return lax.dot_general(
        left, right, (((1,), (1,)), ((), ())), precision=precision, preferred_element_type=jnp.float32
    )


def spread(source, index, place, copies, height):
    picked = source[index]
    width, lanes = picked.shape
    if width == 1:
        tall = jnp.broadcast_to(picked, (height, lanes))
    else:
        tall = jnp.concatenate([picked] * copies, axis=0)
    group = lax.broadcasted_iota(jnp.int32, (height, lanes), 0) // width
    return jnp.where(group == place, tall, 0.0).astype(jnp.bfloat16)


def eliminate(matrix):
    order = matrix.shape[0]
    panel = 8
    at = lax.broadcasted_iota(jnp.int32, (order, LANES), 0)
    lane = lax.broadcasted_iota(jnp.int32, (order, LANES), 1)
    rest = LANES - matrix.shape[1]
    wide = jnp.concatenate([matrix, jnp.zeros((order, rest), jnp.float32)], axis=1)
    wide = jnp.where(lane == at + 2 * order, 1.0, wide)
    for start in range(0, order, panel):
        columns = [
            jnp.broadcast_to(wide[:, k : k + 1], (order, LANES)) for k in range(start, start + panel)
        ]
        for j in range(panel):
            k = start + j
            here = at == k
            column = columns[j]
            inverse = 1.0 / column[k : k + 1]
            for other in range(j + 1, panel):
                row = columns[other][k : k + 1] * inverse
                columns[other] = jnp.where(here, row, columns[other] - column * row)
            row = wide[k : k + 1] * inverse
            wide = jnp.where(here, row, wide - column * row)
    return wide[:, order : order + 1], wide[:, 2 * order : 3 * order]


def kernel(
    cols,
    row_blocks,
    col_blocks,
    brow_hbm,
    bcol_hbm,
    blocks_ref,
    sketch_hbm,
    theta_hbm,
    rhs_hbm,
    out_ref,
    brow_ref,
    bcol_ref,
    sketch_ref,
    theta_ref,
    rhs_ref,
    vals,
    sk_t,
    s_src,
    s_dst,
    zs,
    y_own,
    y_pair,
    y_src,
    y_dst,
    y_all,
    g_plane,
    g_depth,
    xs,
    e_src,
    e_dst,
    zv,
    f_src,
    f_dst,
    h_src,
    h_dst,
    load_sem,
    pair_sem,
    y_sem,
    a_sem,
    g_sem,
    f_sem,
):
    me_r = lax.axis_index("row")
    me_c = lax.axis_index("col")
    stored, order = vals.shape[0], vals.shape[1]
    width = sketch_ref.shape[0]
    pieces = order // LANES
    depth = cols // PLANE
    z, q = me_c // PLANE, me_c % PLANE
    plane = 2 * PLANE
    me_p = me_r * PLANE + q
    core, chip, chips = lax.rem(me_c, 2), me_c // 2, cols // 2
    twin = (me_r, chip * 2 + 1 - core)
    pending = []

    smalls = []
    for at, (src, dst) in enumerate(
        [
            (sketch_hbm, sketch_ref),
            (brow_hbm, brow_ref),
            (bcol_hbm, bcol_ref),
            (theta_hbm, theta_ref),
            (rhs_hbm, rhs_ref),
        ]
    ):
        load = pltpu.make_async_copy(src, dst, load_sem.at[stored + at])
        load.start()
        smalls.append(load)
    loads = []
    for n in range(stored):
        load = pltpu.make_async_copy(blocks_ref.at[n], vals.at[n], load_sem.at[n])
        load.start()
        loads.append(load)

    barrier = pltpu.get_barrier_semaphore()
    for t in range(1, cols):
        pl.semaphore_signal(
            barrier, inc=1, device_id=(me_r, lax.rem(me_c + t, cols)), device_id_type=MESH
        )
    for u in range(PLANE):
        pl.semaphore_signal(
            barrier, inc=1, device_id=(1 - me_r, z * PLANE + u), device_id_type=MESH
        )

    def send(src, dst, sems, at, device):
        copy = pltpu.make_async_remote_copy(
            src_ref=src,
            dst_ref=dst,
            send_sem=sems.at[0, at],
            recv_sem=sems.at[1, at],
            device_id=device,
            device_id_type=MESH,
        )
        copy.start()
        pending.append(copy)
        return copy

    def reduce_start(value, first, sems):
        first[me_p] = value
        copies = []
        for u in range(1, plane):
            peer = lax.rem(me_p + u, plane)
            device = (peer // PLANE, z * PLANE + lax.rem(peer, PLANE))
            copies.append(send(first.at[me_p], first.at[me_p], sems, u - 1, device))
        return copies

    def reduce_middle(copies, first, second, sems):
        for copy in copies:
            copy.wait_recv()
        total = first[0]
        for u in range(1, plane):
            total = total + first[u]
        second[z] = total
        copies = []
        for u in range(1, depth):
            device = (me_r, lax.rem(z + u, depth) * PLANE + q)
            copies.append(send(second.at[z], second.at[z], sems, plane - 2 + u, device))
        return copies

    def reduce_finish(copies, second):
        for copy in copies:
            copy.wait_recv()
        total = second[0]
        for u in range(1, depth):
            total = total + second[u]
        return total

    def scatter_finish(total, copies, dst):
        for t, copy in enumerate(copies, 1):
            copy.wait_recv()
            total = total + dst[t]
        return total

    def strip(ref, j):
        return jnp.concatenate([ref[pieces * j + p : pieces * j + p + 1, :] for p in range(pieces)], axis=1)

    for load in smalls:
        load.wait()
    for i in range(row_blocks):
        sk_t[i] = sketch_ref[:, i * order : (i + 1) * order].astype(jnp.float32)
    own = pl.ds(pl.multiple_of(me_c * LANES, LANES), LANES)
    omega = sketch_ref[:, own].astype(jnp.float32)
    rhs = jnp.broadcast_to(rhs_ref[pl.ds(me_c, 1), :], (8, LANES))

    halves = 2
    half = order // halves
    lefts = [
        spread(sk_t, brow_ref[n], bcol_ref[n], col_blocks, col_blocks * width) for n in range(stored)
    ]
    mine, copies = [], []
    for h in range(halves):
        part = slice(h * half, (h + 1) * half)
        total = jnp.zeros((col_blocks * width, half), jnp.float32)
        for n in range(stored):
            if h == 0:
                loads[n].wait()
            total = total + jnp.dot(lefts[n], vals[n, :, part], preferred_element_type=jnp.float32)
        s_src[h] = total.astype(jnp.bfloat16)
        mine.append(total)
        if h == 0:
            pl.semaphore_wait(barrier, cols - 1 + PLANE)
        copies.append(send(s_src.at[h], s_dst.at[h], pair_sem, h, (1 - me_r, me_c)))
    total = jnp.zeros((row_blocks * width, order), jnp.float32)
    for h in range(halves):
        part = slice(h * half, (h + 1) * half)
        copies[h].wait_recv()
        summed = mine[h] + s_dst[h].astype(jnp.float32)
        for j in range(col_blocks):
            scaled = strip(theta_ref, j)[:, part] * summed[j * width : (j + 1) * width]
            zs[h, j] = scaled.astype(jnp.bfloat16).astype(jnp.float32)
        for n in range(stored):
            left = spread(zs.at[h], bcol_ref[n], brow_ref[n], row_blocks, row_blocks * width)
            total = total + dot_nt(left, vals[n, :, part])
    for i in range(row_blocks):
        for p in range(pieces):
            at = pieces * i + p
            y_own[at % 2, at // 2] = total[i * width : (i + 1) * width, p * LANES : (p + 1) * LANES]
    copy = send(y_own.at[1 - core], y_pair, pair_sem, halves, twin)
    copy.wait_recv()
    for t in range(chips):
        y_src[t] = y_own[core, t] + y_pair[t]
    copies = []
    for t in range(1, chips):
        to = lax.rem(chip + t, chips)
        copies.append(send(y_src.at[to], y_dst.at[t], y_sem, t, (me_r, to * 2 + core)))
    y_t = scatter_finish(y_src[chip] + regularize * omega, copies, y_dst)
    y_all[core, chip] = y_t
    gathers = []
    for t in range(1, chips):
        to = lax.rem(chip + t, chips)
        gathers.append(send(y_all.at[core, chip], y_all.at[core, chip], a_sem, t, (me_r, to * 2 + core)))

    both = y_t + precond_shift * omega
    tall_rhs = jnp.broadcast_to(rhs[:1], (width, LANES))
    upper = jnp.concatenate([0.5 * y_t, 0.5 * both], axis=1)
    lower = jnp.concatenate([jnp.zeros((width, LANES), jnp.float32), tall_rhs], axis=1)
    joined = dot_nt(
        jnp.concatenate([both, y_t], axis=1), jnp.concatenate([upper, lower], axis=0), HIGHEST
    )
    packs = LANES // (2 * width)
    tall = width // packs
    packed = jnp.concatenate([joined[s * tall : (s + 1) * tall] for s in range(packs)], axis=1)
    copies = reduce_start(packed, g_plane, g_sem)
    copies = reduce_middle(copies, g_plane, g_depth, g_sem)
    for copy in gathers:
        copy.wait_recv()
    gathered = send(y_all.at[core], y_all.at[core], a_sem, 0, twin)
    summed = reduce_finish(copies, g_depth)
    joined = jnp.concatenate(
        [summed[:, s * 2 * width : (s + 1) * 2 * width] for s in range(packs)], axis=0
    )
    sketched_rhs = joined[:, width : width + 1]
    coeffs, inverse = eliminate(joined)
    coeffs = jnp.broadcast_to(coeffs, (width, LANES))
    taken = jnp.sum(coeffs * y_t, axis=0, keepdims=True)
    direction = (rhs[:1] - taken) / precond_shift

    gathered.wait_recv()
    lines = []
    for i in range(row_blocks):
        taken = []
        for p in range(pieces):
            at = pieces * i + p
            taken.append(jnp.sum(coeffs * y_all[at % 2, at // 2], axis=0, keepdims=True))
        line = (strip(rhs_ref, i) - jnp.concatenate(taken, axis=1)) / precond_shift
        lines.append(line)
        xs[i] = line.astype(jnp.bfloat16).astype(jnp.float32)
    total = jnp.zeros((16, order), jnp.float32)
    for n in range(stored):
        left = spread(xs, brow_ref[n], bcol_ref[n], col_blocks, 16)
        total = total + jnp.dot(left, vals[n], preferred_element_type=jnp.float32)
    e_src[...] = total[:8]
    copy = send(e_src, e_dst, pair_sem, halves + 1, (1 - me_r, me_c))
    weights = jnp.dot(inverse, y_t, precision=HIGHEST)
    copy.wait_recv()
    image_cols = e_src[...] + e_dst[...]
    for j in range(col_blocks):
        line = (strip(theta_ref, j) * image_cols[j : j + 1]).astype(jnp.bfloat16)
        zv[j] = line.astype(jnp.float32)
    total = jnp.zeros((16, order), jnp.float32)
    for n in range(stored):
        left = spread(zv, bcol_ref[n], brow_ref[n], row_blocks, 16)
        total = total + dot_nt(left, vals[n])

    against = regularize * y_t * direction
    curvature = regularize * direction * direction
    for i in range(row_blocks):
        for p in range(pieces):
            part = slice(p * LANES, (p + 1) * LANES)
            piece = total[i : i + 1, part]
            f_src[pieces * i + p, 0:1] = piece
            against = against + y_all[(pieces * i + p) % 2, (pieces * i + p) // 2] * piece
            curvature = curvature + lines[i][:, part] * piece
    at = lax.broadcasted_iota(jnp.int32, (width, LANES), 0)
    diagonal = lax.broadcasted_iota(jnp.int32, (width, LANES), 1) == at
    against = jnp.where(diagonal, jnp.sum(against, axis=1, keepdims=True), 0.0)
    against = jnp.sum(against, axis=0, keepdims=True)
    curvature = jnp.sum(curvature, axis=1, keepdims=True)
    along = jnp.sum(rhs[:1] * direction, axis=1, keepdims=True)
    lane = lax.broadcasted_iota(jnp.int32, (1, LANES), 1)
    value = jnp.where(lane == width, curvature, jnp.where(lane == width + 1, along, against))
    for to in range(cols):
        f_src[to, 1:2] = value
    copies = []
    for t in range(1, cols):
        to = lax.rem(me_c + t, cols)
        copies.append(send(f_src.at[to], f_dst.at[t], f_sem, t, (me_r, to)))
    gathered = scatter_finish(f_src[me_c], copies, f_dst)
    h_src[...] = gathered
    copy = send(h_src, h_dst, pair_sem, halves + 2, (1 - me_r, me_c))
    image = gathered[0:1]
    copy.wait_recv()
    summed = gathered[1:2] + h_dst[1:2]
    alpha = summed[:, width + 1 : width + 2] / summed[:, width : width + 1]
    sketched = jnp.sum(jnp.where(diagonal, summed, 0.0), axis=1, keepdims=True)
    taken = jnp.sum((sketched_rhs - alpha * sketched) * weights, axis=0, keepdims=True)
    out_ref[0:1] = jnp.broadcast_to(alpha, (1, LANES))
    out_ref[1:2] = direction
    out_ref[2:3] = rhs[:1]
    out_ref[3:4] = image
    out_ref[4:5] = taken
    out_ref[5:8] = jnp.zeros((3, LANES), jnp.float32)
    for copy in pending:
        copy.wait_send()


def fused(cols, blocks, block_rows, block_cols, sketch, theta, rhs):
    stored, order = blocks.shape[2], blocks.shape[3]
    local, width = sketch.shape
    row_blocks = local // order
    col_blocks = theta.shape[0] // order
    depth = cols // PLANE
    vmem = pl.BlockSpec(memory_space=pltpu.VMEM)
    hbm = pl.BlockSpec(memory_space=pl.ANY)
    f32, bf16 = jnp.float32, jnp.bfloat16
    reduce_sems = pltpu.SemaphoreType.DMA((2, 2 * PLANE + depth))
    col_sems = pltpu.SemaphoreType.DMA((2, cols))
    out = pl.pallas_call(
        functools.partial(kernel, cols, row_blocks, col_blocks),
        out_shape=jax.ShapeDtypeStruct((8, LANES), jnp.float32),
        in_specs=[hbm] * 6,
        out_specs=vmem,
        scratch_shapes=[
            pltpu.SMEM((stored,), jnp.int32),
            pltpu.SMEM((stored,), jnp.int32),
            pltpu.VMEM((width, local), bf16),
            pltpu.VMEM((theta.shape[0] // LANES, LANES), f32),
            pltpu.VMEM((local // LANES, LANES), f32),
            pltpu.VMEM((stored, order, order), bf16),
            pltpu.VMEM((row_blocks, width, order), f32),
            pltpu.VMEM((2, col_blocks * width, order // 2), bf16),
            pltpu.VMEM((2, col_blocks * width, order // 2), bf16),
            pltpu.VMEM((2, col_blocks, width, order // 2), f32),
            pltpu.VMEM((2, cols // 2, width, LANES), f32),
            pltpu.VMEM((cols // 2, width, LANES), f32),
            pltpu.VMEM((cols // 2, width, LANES), f32),
            pltpu.VMEM((cols // 2, width, LANES), f32),
            pltpu.VMEM((2, cols // 2, width, LANES), f32),
            pltpu.VMEM((2 * PLANE, 16, LANES), f32),
            pltpu.VMEM((depth, 16, LANES), f32),
            pltpu.VMEM((row_blocks, 1, order), f32),
            pltpu.VMEM((8, order), f32),
            pltpu.VMEM((8, order), f32),
            pltpu.VMEM((col_blocks, 1, order), f32),
            pltpu.VMEM((cols, 2, LANES), f32),
            pltpu.VMEM((cols, 2, LANES), f32),
            pltpu.VMEM((2, LANES), f32),
            pltpu.VMEM((2, LANES), f32),
            pltpu.SemaphoreType.DMA((stored + 5,)),
            pltpu.SemaphoreType.DMA((2, 5)),
            col_sems,
            col_sems,
            reduce_sems,
            col_sems,
        ],
        compiler_params=pltpu.CompilerParams(
            collective_id=0, has_side_effects=True, vmem_limit_bytes=VMEM_BYTES
        ),
    )(
        block_rows.reshape(stored),
        block_cols.reshape(stored),
        blocks.reshape(stored, order, order),
        sketch.T,
        theta.reshape(-1, LANES),
        rhs.reshape(-1, LANES),
    )
    alpha, direction, mine, image, taken = (out[i] for i in range(5))
    iterate = alpha * direction
    residual = mine - alpha * image - regularize * iterate
    return iterate, residual, (residual - taken) / precond_shift


def tile_transpose(values, rows_idx, cols_idx, inputs, col_count):
    order = values.shape[1]
    width = inputs.shape[1]
    picked = inputs.reshape(-1, order, width)[rows_idx]
    product = jnp.einsum("nab,nak->nbk", values, picked, preferred_element_type=jnp.float32)
    onehot = (cols_idx[:, None] == jnp.arange(col_count, dtype=jnp.int32)[None, :]).astype(
        jnp.float32
    )
    merged = jnp.einsum("nj,nbk->jbk", onehot, product, precision=lax.Precision.HIGHEST)
    return merged.reshape(col_count * order, width)


def tile_forward(values, rows_idx, cols_idx, inputs, row_count):
    order = values.shape[1]
    width = inputs.shape[1]
    picked = inputs.reshape(-1, order, width)[cols_idx]
    product = jnp.einsum("nab,nbk->nak", values, picked, preferred_element_type=jnp.float32)
    onehot = (rows_idx[:, None] == jnp.arange(row_count, dtype=jnp.int32)[None, :]).astype(
        jnp.float32
    )
    merged = jnp.einsum("ni,nak->iak", onehot, product, precision=lax.Precision.HIGHEST)
    return merged.reshape(row_count * order, width)


def solve_gram(factor, vector):
    middle = lax.linalg.triangular_solve(factor, vector[:, None], left_side=True, lower=True)
    result = lax.linalg.triangular_solve(
        factor, middle, left_side=True, lower=True, transpose_a=True
    )
    return result[:, 0]


def shards(blocks, block_rows, block_cols, sketch, theta, rhs):
    values = blocks[0, 0]
    rows_idx = block_rows[0, 0]
    cols_idx = block_cols[0, 0]
    order = values.shape[1]
    local_rows = sketch.shape[0]
    row_count = local_rows // order
    col_count = theta.shape[0] // order
    share = local_rows // lax.axis_size("col")
    offset = lax.axis_index("col") * share
    sketch_f = sketch.astype(jnp.float32)
    sketch_part = lax.dynamic_slice_in_dim(sketch_f, offset, share, 0)
    rhs_part = lax.dynamic_slice_in_dim(rhs, offset, share, 0)
    col_terms = tile_transpose(values, rows_idx, cols_idx, sketch, col_count)
    sketch_cols = lax.psum(col_terms, "row")
    scaled = (theta[:, None] * sketch_cols).astype(jnp.bfloat16)
    row_terms = tile_forward(values, rows_idx, cols_idx, scaled, row_count)
    ysketch = lax.psum(row_terms, "col") + regularize * sketch_f
    y_part = lax.dynamic_slice_in_dim(ysketch, offset, share, 0)
    cross = jnp.dot(sketch_part.T, y_part, precision=lax.Precision.HIGHEST)
    gram_terms = precond_shift * 0.5 * (cross + cross.T) + jnp.dot(
        y_part.T, y_part, precision=lax.Precision.HIGHEST
    )
    yb_terms = jnp.dot(rhs_part, y_part, precision=lax.Precision.HIGHEST)
    gram, sketched_rhs = lax.psum((gram_terms, yb_terms), ("row", "col"))
    factor = jnp.linalg.cholesky(gram)
    coeffs = solve_gram(factor, sketched_rhs)
    direction_full = (
        rhs - jnp.dot(ysketch, coeffs, precision=lax.Precision.HIGHEST)
    ) / precond_shift
    direction = lax.dynamic_slice_in_dim(direction_full, offset, share, 0)
    dir_low = direction_full.astype(jnp.bfloat16)
    image_terms = tile_transpose(values, rows_idx, cols_idx, dir_low[:, None], col_count)[:, 0]
    image_cols = lax.psum(image_terms, "row")
    image_scaled = (theta * image_cols).astype(jnp.bfloat16)
    product_terms = tile_forward(values, rows_idx, cols_idx, image_scaled[:, None], row_count)[:, 0]
    image_full = lax.psum(product_terms, "col")
    image = lax.dynamic_slice_in_dim(image_full, offset, share, 0) + regularize * direction
    along = lax.psum(jnp.sum(rhs_part * direction), ("row", "col"))
    curvature = lax.psum(jnp.sum(direction * image), ("row", "col"))
    alpha = along / curvature
    residual = rhs_part - alpha * image
    sketched_res = lax.psum(
        jnp.dot(residual, y_part, precision=lax.Precision.HIGHEST), ("row", "col")
    )
    solution = alpha * direction
    res_coeffs = solve_gram(factor, sketched_res)
    precond_residual = (
        residual - jnp.dot(y_part, res_coeffs, precision=lax.Precision.HIGHEST)
    ) / precond_shift
    return (solution, residual, precond_residual)


def solution(mesh):
    in_specs = (
        P("row", "col", None, None, None),
        P("row", "col", None),
        P("row", "col", None),
        P("row", None),
        P("col"),
        P("row"),
    )
    out_specs = (P(("row", "col")), P(("row", "col")), P(("row", "col")))
    cols = mesh.shape["col"]

    def step(blocks, block_rows, block_cols, sketch, theta, rhs):
        share = sketch.shape[0] // cols
        if mesh.shape["row"] == 2 and cols % PLANE == 0 and share == LANES:
            return fused(cols, blocks, block_rows, block_cols, sketch, theta, rhs)
        return shards(blocks, block_rows, block_cols, sketch, theta, rhs)

    return jax.shard_map(step, mesh=mesh, in_specs=in_specs, out_specs=out_specs, check_vma=False)
```

```python
import functools

import jax
import jax.numpy as jnp
from jax import lax
from jax.experimental import pallas as pl
from jax.experimental.pallas import tpu as pltpu
from jax.sharding import PartitionSpec as P

precond_shift = 1.0
regularize = 0.5
MESH = pl.DeviceIdType.MESH
HIGHEST = lax.Precision.HIGHEST
PLANE = 4
LANES = 128
VMEM_BYTES = 64 * 1024 * 1024


def dot_nt(left, right, precision=None):
    return lax.dot_general(
        left, right, (((1,), (1,)), ((), ())), precision=precision, preferred_element_type=jnp.float32
    )


def spread(source, index, place, copies, height):
    picked = source[index]
    width, lanes = picked.shape
    if width == 1:
        tall = jnp.broadcast_to(picked, (height, lanes))
    else:
        tall = jnp.concatenate([picked] * copies, axis=0)
    group = lax.broadcasted_iota(jnp.int32, (height, lanes), 0) // width
    return jnp.where(group == place, tall, 0.0).astype(jnp.bfloat16)


def spread_lanes(source, index, place, width):
    picked = source[index]
    group = lax.broadcasted_iota(jnp.int32, picked.shape, 1) // width
    return jnp.where(group == place, picked, 0.0).astype(jnp.bfloat16)


def eliminate(matrix):
    order = matrix.shape[0]
    panel = 8
    at = lax.broadcasted_iota(jnp.int32, (order, LANES), 0)
    lane = lax.broadcasted_iota(jnp.int32, (order, LANES), 1)
    rest = LANES - matrix.shape[1]
    wide = jnp.concatenate([matrix, jnp.zeros((order, rest), jnp.float32)], axis=1)
    wide = jnp.where(lane == at + 2 * order, 1.0, wide)
    for start in range(0, order, panel):
        columns = [
            jnp.broadcast_to(wide[:, k : k + 1], (order, LANES)) for k in range(start, start + panel)
        ]
        for j in range(panel):
            k = start + j
            here = at == k
            column = columns[j]
            inverse = 1.0 / column[k : k + 1]
            for other in range(j + 1, panel):
                row = columns[other][k : k + 1] * inverse
                columns[other] = jnp.where(here, row, columns[other] - column * row)
            row = wide[k : k + 1] * inverse
            wide = jnp.where(here, row, wide - column * row)
    return wide[:, order : order + 1], wide[:, 2 * order : 3 * order]


def kernel(
    cols,
    row_blocks,
    col_blocks,
    brow_hbm,
    bcol_hbm,
    blocks_ref,
    sketch_hbm,
    theta_hbm,
    rhs_hbm,
    out_ref,
    brow_ref,
    bcol_ref,
    sketch_ref,
    theta_ref,
    rhs_ref,
    vals,
    sk_t,
    s_src,
    s_dst,
    zs,
    y_own,
    y_pair,
    y_src,
    y_dst,
    y_all,
    g_plane,
    g_depth,
    xs,
    e_src,
    e_dst,
    zv,
    f_src,
    f_dst,
    h_src,
    h_dst,
    load_sem,
    pair_sem,
    y_sem,
    a_sem,
    g_sem,
    f_sem,
):
    me_r = lax.axis_index("row")
    me_c = lax.axis_index("col")
    stored, order = vals.shape[0], vals.shape[1]
    width = sketch_ref.shape[0]
    pieces = order // LANES
    depth = cols // PLANE
    z, q = me_c // PLANE, me_c % PLANE
    plane = 2 * PLANE
    me_p = me_r * PLANE + q
    core, chip, chips = lax.rem(me_c, 2), me_c // 2, cols // 2
    twin = (me_r, chip * 2 + 1 - core)
    pending = []

    smalls = []
    for at, (src, dst) in enumerate(
        [
            (sketch_hbm, sketch_ref),
            (brow_hbm, brow_ref),
            (bcol_hbm, bcol_ref),
            (theta_hbm, theta_ref),
            (rhs_hbm, rhs_ref),
        ]
    ):
        load = pltpu.make_async_copy(src, dst, load_sem.at[stored + at])
        load.start()
        smalls.append(load)
    loads = []
    for n in range(stored):
        load = pltpu.make_async_copy(blocks_ref.at[n], vals.at[n], load_sem.at[n])
        load.start()
        loads.append(load)

    barrier = pltpu.get_barrier_semaphore()
    for t in range(1, cols):
        pl.semaphore_signal(
            barrier, inc=1, device_id=(me_r, lax.rem(me_c + t, cols)), device_id_type=MESH
        )
    for u in range(PLANE):
        pl.semaphore_signal(
            barrier, inc=1, device_id=(1 - me_r, z * PLANE + u), device_id_type=MESH
        )

    def send(src, dst, sems, at, device):
        copy = pltpu.make_async_remote_copy(
            src_ref=src,
            dst_ref=dst,
            send_sem=sems.at[0, at],
            recv_sem=sems.at[1, at],
            device_id=device,
            device_id_type=MESH,
        )
        copy.start()
        pending.append(copy)
        return copy

    def reduce_start(value, first, sems):
        first[me_p] = value
        copies = []
        for u in range(1, plane):
            peer = lax.rem(me_p + u, plane)
            device = (peer // PLANE, z * PLANE + lax.rem(peer, PLANE))
            copies.append(send(first.at[me_p], first.at[me_p], sems, u - 1, device))
        return copies

    def reduce_middle(copies, first, second, sems):
        for copy in copies:
            copy.wait_recv()
        total = first[0]
        for u in range(1, plane):
            total = total + first[u]
        second[z] = total
        copies = []
        for u in range(1, depth):
            device = (me_r, lax.rem(z + u, depth) * PLANE + q)
            copies.append(send(second.at[z], second.at[z], sems, plane - 2 + u, device))
        return copies

    def reduce_finish(copies, second):
        for copy in copies:
            copy.wait_recv()
        total = second[0]
        for u in range(1, depth):
            total = total + second[u]
        return total

    def scatter_finish(total, copies, dst):
        for t, copy in enumerate(copies, 1):
            copy.wait_recv()
            total = total + dst[t]
        return total

    def strip(ref, j):
        return jnp.concatenate([ref[pieces * j + p : pieces * j + p + 1, :] for p in range(pieces)], axis=1)

    for load in smalls:
        load.wait()
    for i in range(row_blocks):
        sk_t[i] = sketch_ref[:, i * order : (i + 1) * order].astype(jnp.float32)
    own = pl.ds(pl.multiple_of(me_c * LANES, LANES), LANES)
    omega = sketch_ref[:, own].astype(jnp.float32)
    rhs = jnp.broadcast_to(rhs_ref[pl.ds(me_c, 1), :], (8, LANES))

    halves = 2
    half = order // halves
    lefts = [
        spread(sk_t, brow_ref[n], bcol_ref[n], col_blocks, col_blocks * width) for n in range(stored)
    ]
    mine, copies = [], []
    for h in range(halves):
        part = slice(h * half, (h + 1) * half)
        total = jnp.zeros((col_blocks * width, half), jnp.float32)
        for n in range(stored):
            if h == 0:
                loads[n].wait()
            total = total + jnp.dot(lefts[n], vals[n, :, part], preferred_element_type=jnp.float32)
        s_src[h] = total.astype(jnp.bfloat16)
        mine.append(total)
        if h == 0:
            pl.semaphore_wait(barrier, cols - 1 + PLANE)
        copies.append(send(s_src.at[h], s_dst.at[h], pair_sem, h, (1 - me_r, me_c)))
    total = jnp.zeros((order, row_blocks * width), jnp.float32)
    for h in range(halves):
        part = slice(h * half, (h + 1) * half)
        copies[h].wait_recv()
        summed = mine[h] + s_dst[h].astype(jnp.float32)
        for j in range(col_blocks):
            scaled = strip(theta_ref, j)[:, part] * summed[j * width : (j + 1) * width]
            scaled = scaled.astype(jnp.bfloat16).astype(jnp.float32)
            zs[h, j] = jnp.concatenate([scaled] * row_blocks, axis=0).T
        for n in range(stored):
            right = spread_lanes(zs.at[h], bcol_ref[n], brow_ref[n], width)
            total = total + jnp.dot(vals[n, :, part], right, preferred_element_type=jnp.float32)
    for p in range(pieces):
        turned = total[p * LANES : (p + 1) * LANES].T
        for i in range(row_blocks):
            at = pieces * i + p
            y_own[at % 2, at // 2] = turned[i * width : (i + 1) * width]
    copy = send(y_own.at[1 - core], y_pair, pair_sem, halves, twin)
    copy.wait_recv()
    for t in range(chips):
        y_src[t] = y_own[core, t] + y_pair[t]
    copies = []
    for t in range(1, chips):
        to = lax.rem(chip + t, chips)
        copies.append(send(y_src.at[to], y_dst.at[t], y_sem, t, (me_r, to * 2 + core)))
    y_t = scatter_finish(y_src[chip] + regularize * omega, copies, y_dst)
    y_all[core, chip] = y_t
    gathers = []
    for t in range(1, chips):
        to = lax.rem(chip + t, chips)
        gathers.append(send(y_all.at[core, chip], y_all.at[core, chip], a_sem, t, (me_r, to * 2 + core)))

    both = y_t + precond_shift * omega
    tall_rhs = jnp.broadcast_to(rhs[:1], (width, LANES))
    upper = jnp.concatenate([0.5 * y_t, 0.5 * both], axis=1)
    lower = jnp.concatenate([jnp.zeros((width, LANES), jnp.float32), tall_rhs], axis=1)
    joined = dot_nt(
        jnp.concatenate([both, y_t], axis=1), jnp.concatenate([upper, lower], axis=0), HIGHEST
    )
    packs = LANES // (2 * width)
    tall = width // packs
    packed = jnp.concatenate([joined[s * tall : (s + 1) * tall] for s in range(packs)], axis=1)
    copies = reduce_start(packed, g_plane, g_sem)
    copies = reduce_middle(copies, g_plane, g_depth, g_sem)
    for copy in gathers:
        copy.wait_recv()
    gathered = send(y_all.at[core], y_all.at[core], a_sem, 0, twin)
    summed = reduce_finish(copies, g_depth)
    joined = jnp.concatenate(
        [summed[:, s * 2 * width : (s + 1) * 2 * width] for s in range(packs)], axis=0
    )
    sketched_rhs = joined[:, width : width + 1]
    coeffs, inverse = eliminate(joined)
    coeffs = jnp.broadcast_to(coeffs, (width, LANES))
    taken = jnp.sum(coeffs * y_t, axis=0, keepdims=True)
    direction = (rhs[:1] - taken) / precond_shift

    gathered.wait_recv()
    lines = []
    for i in range(row_blocks):
        taken = []
        for p in range(pieces):
            at = pieces * i + p
            taken.append(jnp.sum(coeffs * y_all[at % 2, at // 2], axis=0, keepdims=True))
        line = (strip(rhs_ref, i) - jnp.concatenate(taken, axis=1)) / precond_shift
        lines.append(line)
        xs[i] = line.astype(jnp.bfloat16).astype(jnp.float32)
    total = jnp.zeros((16, order), jnp.float32)
    for n in range(stored):
        left = spread(xs, brow_ref[n], bcol_ref[n], col_blocks, 16)
        total = total + jnp.dot(left, vals[n], preferred_element_type=jnp.float32)
    e_src[...] = total[:8]
    copy = send(e_src, e_dst, pair_sem, halves + 1, (1 - me_r, me_c))
    weights = jnp.dot(inverse, y_t, precision=HIGHEST)
    copy.wait_recv()
    image_cols = e_src[...] + e_dst[...]
    for j in range(col_blocks):
        line = (strip(theta_ref, j) * image_cols[j : j + 1]).astype(jnp.bfloat16)
        zv[j] = jnp.broadcast_to(line.astype(jnp.float32), (LANES, order)).T
    total = jnp.zeros((order, LANES), jnp.float32)
    for n in range(stored):
        right = spread_lanes(zv, bcol_ref[n], brow_ref[n], width)
        total = total + jnp.dot(vals[n], right, preferred_element_type=jnp.float32)
    turned = [total[p * LANES : (p + 1) * LANES].T for p in range(pieces)]

    against = regularize * y_t * direction
    curvature = regularize * direction * direction
    for i in range(row_blocks):
        for p in range(pieces):
            part = slice(p * LANES, (p + 1) * LANES)
            piece = turned[p][i * width : i * width + 1]
            f_src[pieces * i + p, 0:1] = piece
            against = against + y_all[(pieces * i + p) % 2, (pieces * i + p) // 2] * piece
            curvature = curvature + lines[i][:, part] * piece
    at = lax.broadcasted_iota(jnp.int32, (width, LANES), 0)
    diagonal = lax.broadcasted_iota(jnp.int32, (width, LANES), 1) == at
    against = jnp.where(diagonal, jnp.sum(against, axis=1, keepdims=True), 0.0)
    against = jnp.sum(against, axis=0, keepdims=True)
    curvature = jnp.sum(curvature, axis=1, keepdims=True)
    along = jnp.sum(rhs[:1] * direction, axis=1, keepdims=True)
    lane = lax.broadcasted_iota(jnp.int32, (1, LANES), 1)
    value = jnp.where(lane == width, curvature, jnp.where(lane == width + 1, along, against))
    for to in range(cols):
        f_src[to, 1:2] = value
    copies = []
    for t in range(1, cols):
        to = lax.rem(me_c + t, cols)
        copies.append(send(f_src.at[to], f_dst.at[t], f_sem, t, (me_r, to)))
    gathered = scatter_finish(f_src[me_c], copies, f_dst)
    h_src[...] = gathered
    copy = send(h_src, h_dst, pair_sem, halves + 2, (1 - me_r, me_c))
    image = gathered[0:1]
    copy.wait_recv()
    summed = gathered[1:2] + h_dst[1:2]
    alpha = summed[:, width + 1 : width + 2] / summed[:, width : width + 1]
    sketched = jnp.sum(jnp.where(diagonal, summed, 0.0), axis=1, keepdims=True)
    taken = jnp.sum((sketched_rhs - alpha * sketched) * weights, axis=0, keepdims=True)
    out_ref[0:1] = jnp.broadcast_to(alpha, (1, LANES))
    out_ref[1:2] = direction
    out_ref[2:3] = rhs[:1]
    out_ref[3:4] = image
    out_ref[4:5] = taken
    out_ref[5:8] = jnp.zeros((3, LANES), jnp.float32)
    for copy in pending:
        copy.wait_send()


def fused(cols, blocks, block_rows, block_cols, sketch, theta, rhs):
    stored, order = blocks.shape[2], blocks.shape[3]
    local, width = sketch.shape
    row_blocks = local // order
    col_blocks = theta.shape[0] // order
    depth = cols // PLANE
    vmem = pl.BlockSpec(memory_space=pltpu.VMEM)
    hbm = pl.BlockSpec(memory_space=pl.ANY)
    f32, bf16 = jnp.float32, jnp.bfloat16
    reduce_sems = pltpu.SemaphoreType.DMA((2, 2 * PLANE + depth))
    col_sems = pltpu.SemaphoreType.DMA((2, cols))
    out = pl.pallas_call(
        functools.partial(kernel, cols, row_blocks, col_blocks),
        out_shape=jax.ShapeDtypeStruct((8, LANES), jnp.float32),
        in_specs=[hbm] * 6,
        out_specs=vmem,
        scratch_shapes=[
            pltpu.SMEM((stored,), jnp.int32),
            pltpu.SMEM((stored,), jnp.int32),
            pltpu.VMEM((width, local), bf16),
            pltpu.VMEM((theta.shape[0] // LANES, LANES), f32),
            pltpu.VMEM((local // LANES, LANES), f32),
            pltpu.VMEM((stored, order, order), bf16),
            pltpu.VMEM((row_blocks, width, order), f32),
            pltpu.VMEM((2, col_blocks * width, order // 2), bf16),
            pltpu.VMEM((2, col_blocks * width, order // 2), bf16),
            pltpu.VMEM((2, col_blocks, order // 2, row_blocks * width), f32),
            pltpu.VMEM((2, cols // 2, width, LANES), f32),
            pltpu.VMEM((cols // 2, width, LANES), f32),
            pltpu.VMEM((cols // 2, width, LANES), f32),
            pltpu.VMEM((cols // 2, width, LANES), f32),
            pltpu.VMEM((2, cols // 2, width, LANES), f32),
            pltpu.VMEM((2 * PLANE, 16, LANES), f32),
            pltpu.VMEM((depth, 16, LANES), f32),
            pltpu.VMEM((row_blocks, 1, order), f32),
            pltpu.VMEM((8, order), f32),
            pltpu.VMEM((8, order), f32),
            pltpu.VMEM((col_blocks, order, LANES), f32),
            pltpu.VMEM((cols, 2, LANES), f32),
            pltpu.VMEM((cols, 2, LANES), f32),
            pltpu.VMEM((2, LANES), f32),
            pltpu.VMEM((2, LANES), f32),
            pltpu.SemaphoreType.DMA((stored + 5,)),
            pltpu.SemaphoreType.DMA((2, 5)),
            col_sems,
            col_sems,
            reduce_sems,
            col_sems,
        ],
        compiler_params=pltpu.CompilerParams(
            collective_id=0, has_side_effects=True, vmem_limit_bytes=VMEM_BYTES
        ),
    )(
        block_rows.reshape(stored),
        block_cols.reshape(stored),
        blocks.reshape(stored, order, order),
        sketch.T,
        theta.reshape(-1, LANES),
        rhs.reshape(-1, LANES),
    )
    alpha, direction, mine, image, taken = (out[i] for i in range(5))
    iterate = alpha * direction
    residual = mine - alpha * image - regularize * iterate
    return iterate, residual, (residual - taken) / precond_shift


def tile_transpose(values, rows_idx, cols_idx, inputs, col_count):
    order = values.shape[1]
    width = inputs.shape[1]
    picked = inputs.reshape(-1, order, width)[rows_idx]
    product = jnp.einsum("nab,nak->nbk", values, picked, preferred_element_type=jnp.float32)
    onehot = (cols_idx[:, None] == jnp.arange(col_count, dtype=jnp.int32)[None, :]).astype(
        jnp.float32
    )
    merged = jnp.einsum("nj,nbk->jbk", onehot, product, precision=lax.Precision.HIGHEST)
    return merged.reshape(col_count * order, width)


def tile_forward(values, rows_idx, cols_idx, inputs, row_count):
    order = values.shape[1]
    width = inputs.shape[1]
    picked = inputs.reshape(-1, order, width)[cols_idx]
    product = jnp.einsum("nab,nbk->nak", values, picked, preferred_element_type=jnp.float32)
    onehot = (rows_idx[:, None] == jnp.arange(row_count, dtype=jnp.int32)[None, :]).astype(
        jnp.float32
    )
    merged = jnp.einsum("ni,nak->iak", onehot, product, precision=lax.Precision.HIGHEST)
    return merged.reshape(row_count * order, width)


def solve_gram(factor, vector):
    middle = lax.linalg.triangular_solve(factor, vector[:, None], left_side=True, lower=True)
    result = lax.linalg.triangular_solve(
        factor, middle, left_side=True, lower=True, transpose_a=True
    )
    return result[:, 0]


def shards(blocks, block_rows, block_cols, sketch, theta, rhs):
    values = blocks[0, 0]
    rows_idx = block_rows[0, 0]
    cols_idx = block_cols[0, 0]
    order = values.shape[1]
    local_rows = sketch.shape[0]
    row_count = local_rows // order
    col_count = theta.shape[0] // order
    share = local_rows // lax.axis_size("col")
    offset = lax.axis_index("col") * share
    sketch_f = sketch.astype(jnp.float32)
    sketch_part = lax.dynamic_slice_in_dim(sketch_f, offset, share, 0)
    rhs_part = lax.dynamic_slice_in_dim(rhs, offset, share, 0)
    col_terms = tile_transpose(values, rows_idx, cols_idx, sketch, col_count)
    sketch_cols = lax.psum(col_terms, "row")
    scaled = (theta[:, None] * sketch_cols).astype(jnp.bfloat16)
    row_terms = tile_forward(values, rows_idx, cols_idx, scaled, row_count)
    ysketch = lax.psum(row_terms, "col") + regularize * sketch_f
    y_part = lax.dynamic_slice_in_dim(ysketch, offset, share, 0)
    cross = jnp.dot(sketch_part.T, y_part, precision=lax.Precision.HIGHEST)
    gram_terms = precond_shift * 0.5 * (cross + cross.T) + jnp.dot(
        y_part.T, y_part, precision=lax.Precision.HIGHEST
    )
    yb_terms = jnp.dot(rhs_part, y_part, precision=lax.Precision.HIGHEST)
    gram, sketched_rhs = lax.psum((gram_terms, yb_terms), ("row", "col"))
    factor = jnp.linalg.cholesky(gram)
    coeffs = solve_gram(factor, sketched_rhs)
    direction_full = (
        rhs - jnp.dot(ysketch, coeffs, precision=lax.Precision.HIGHEST)
    ) / precond_shift
    direction = lax.dynamic_slice_in_dim(direction_full, offset, share, 0)
    dir_low = direction_full.astype(jnp.bfloat16)
    image_terms = tile_transpose(values, rows_idx, cols_idx, dir_low[:, None], col_count)[:, 0]
    image_cols = lax.psum(image_terms, "row")
    image_scaled = (theta * image_cols).astype(jnp.bfloat16)
    product_terms = tile_forward(values, rows_idx, cols_idx, image_scaled[:, None], row_count)[:, 0]
    image_full = lax.psum(product_terms, "col")
    image = lax.dynamic_slice_in_dim(image_full, offset, share, 0) + regularize * direction
    along = lax.psum(jnp.sum(rhs_part * direction), ("row", "col"))
    curvature = lax.psum(jnp.sum(direction * image), ("row", "col"))
    alpha = along / curvature
    residual = rhs_part - alpha * image
    sketched_res = lax.psum(
        jnp.dot(residual, y_part, precision=lax.Precision.HIGHEST), ("row", "col")
    )
    solution = alpha * direction
    res_coeffs = solve_gram(factor, sketched_res)
    precond_residual = (
        residual - jnp.dot(y_part, res_coeffs, precision=lax.Precision.HIGHEST)
    ) / precond_shift
    return (solution, residual, precond_residual)


def solution(mesh):
    in_specs = (
        P("row", "col", None, None, None),
        P("row", "col", None),
        P("row", "col", None),
        P("row", None),
        P("col"),
        P("row"),
    )
    out_specs = (P(("row", "col")), P(("row", "col")), P(("row", "col")))
    cols = mesh.shape["col"]

    def step(blocks, block_rows, block_cols, sketch, theta, rhs):
        share = sketch.shape[0] // cols
        if mesh.shape["row"] == 2 and cols % PLANE == 0 and share == LANES:
            return fused(cols, blocks, block_rows, block_cols, sketch, theta, rhs)
        return shards(blocks, block_rows, block_cols, sketch, theta, rhs)

    return jax.shard_map(step, mesh=mesh, in_specs=in_specs, out_specs=out_specs, check_vma=False)
```

```python
import functools

import jax
import jax.numpy as jnp
from jax import lax
from jax.experimental import pallas as pl
from jax.experimental.pallas import tpu as pltpu
from jax.sharding import PartitionSpec as P

precond_shift = 1.0
regularize = 0.5
MESH = pl.DeviceIdType.MESH
HIGHEST = lax.Precision.HIGHEST
PLANE = 4
LANES = 128
VMEM_BYTES = 64 * 1024 * 1024


def dot_nt(left, right, precision=None):
    return lax.dot_general(
        left, right, (((1,), (1,)), ((), ())), precision=precision, preferred_element_type=jnp.float32
    )


def spread(source, index, place, copies, height):
    picked = source[index]
    width, lanes = picked.shape
    if width == 1:
        tall = jnp.broadcast_to(picked, (height, lanes))
    else:
        tall = jnp.concatenate([picked] * copies, axis=0)
    group = lax.broadcasted_iota(jnp.int32, (height, lanes), 0) // width
    return jnp.where(group == place, tall, 0.0).astype(jnp.bfloat16)


def eliminate(matrix):
    order = matrix.shape[0]
    panel = 8
    at = lax.broadcasted_iota(jnp.int32, (order, LANES), 0)
    lane = lax.broadcasted_iota(jnp.int32, (order, LANES), 1)
    rest = LANES - matrix.shape[1]
    wide = jnp.concatenate([matrix, jnp.zeros((order, rest), jnp.float32)], axis=1)
    wide = jnp.where(lane == at + 2 * order, 1.0, wide)
    for start in range(0, order, panel):
        columns = [
            jnp.broadcast_to(wide[:, k : k + 1], (order, LANES)) for k in range(start, start + panel)
        ]
        for j in range(panel):
            k = start + j
            here = at == k
            column = columns[j]
            inverse = 1.0 / column[k : k + 1]
            for other in range(j + 1, panel):
                row = columns[other][k : k + 1] * inverse
                columns[other] = jnp.where(here, row, columns[other] - column * row)
            row = wide[k : k + 1] * inverse
            wide = jnp.where(here, row, wide - column * row)
    return wide[:, order : order + 1], wide[:, 2 * order : 3 * order]


def kernel(
    cols,
    row_blocks,
    col_blocks,
    brow_hbm,
    bcol_hbm,
    blocks_ref,
    sketch_hbm,
    theta_hbm,
    rhs_hbm,
    out_ref,
    brow_ref,
    bcol_ref,
    sketch_ref,
    theta_ref,
    rhs_ref,
    vals,
    sk_t,
    s_src,
    s_dst,
    zs,
    y_own,
    y_pair,
    y_src,
    y_dst,
    y_all,
    g_plane,
    g_depth,
    xs,
    e_src,
    e_dst,
    zv,
    f_src,
    f_dst,
    h_src,
    h_dst,
    load_sem,
    pair_sem,
    y_sem,
    a_sem,
    g_sem,
    f_sem,
    h_sem,
):
    me_r = lax.axis_index("row")
    me_c = lax.axis_index("col")
    stored, order = vals.shape[0], vals.shape[1]
    width = sketch_ref.shape[0]
    pieces = order // LANES
    depth = cols // PLANE
    z, q = me_c // PLANE, me_c % PLANE
    plane = 2 * PLANE
    me_p = me_r * PLANE + q
    core, chip, chips = lax.rem(me_c, 2), me_c // 2, cols // 2
    twin = (me_r, chip * 2 + 1 - core)
    pending = []

    smalls = []
    for at, (src, dst) in enumerate(
        [
            (sketch_hbm, sketch_ref),
            (brow_hbm, brow_ref),
            (bcol_hbm, bcol_ref),
            (theta_hbm, theta_ref),
            (rhs_hbm, rhs_ref),
        ]
    ):
        load = pltpu.make_async_copy(src, dst, load_sem.at[stored + at])
        load.start()
        smalls.append(load)
    loads = []
    for n in range(stored):
        load = pltpu.make_async_copy(blocks_ref.at[n], vals.at[n], load_sem.at[n])
        load.start()
        loads.append(load)

    barrier = pltpu.get_barrier_semaphore()
    for t in range(1, cols):
        pl.semaphore_signal(
            barrier, inc=1, device_id=(me_r, lax.rem(me_c + t, cols)), device_id_type=MESH
        )
    for t in range(cols):
        pl.semaphore_signal(
            barrier, inc=1, device_id=(1 - me_r, lax.rem(me_c + t, cols)), device_id_type=MESH
        )

    def send(src, dst, sems, at, device):
        copy = pltpu.make_async_remote_copy(
            src_ref=src,
            dst_ref=dst,
            send_sem=sems.at[0, at],
            recv_sem=sems.at[1, at],
            device_id=device,
            device_id_type=MESH,
        )
        copy.start()
        pending.append(copy)
        return copy

    def reduce_start(value, first, sems):
        first[me_p] = value
        copies = []
        for u in range(1, plane):
            peer = lax.rem(me_p + u, plane)
            device = (peer // PLANE, z * PLANE + lax.rem(peer, PLANE))
            copies.append(send(first.at[me_p], first.at[me_p], sems, u - 1, device))
        return copies

    def reduce_middle(copies, first, second, sems):
        for copy in copies:
            copy.wait_recv()
        total = first[0]
        for u in range(1, plane):
            total = total + first[u]
        second[z] = total
        copies = []
        for u in range(1, depth):
            device = (me_r, lax.rem(z + u, depth) * PLANE + q)
            copies.append(send(second.at[z], second.at[z], sems, plane - 2 + u, device))
        return copies

    def reduce_finish(copies, second):
        for copy in copies:
            copy.wait_recv()
        total = second[0]
        for u in range(1, depth):
            total = total + second[u]
        return total

    def scatter_finish(total, copies, dst):
        for t, copy in enumerate(copies, 1):
            copy.wait_recv()
            total = total + dst[t]
        return total

    def strip(ref, j):
        return jnp.concatenate([ref[pieces * j + p : pieces * j + p + 1, :] for p in range(pieces)], axis=1)

    for load in smalls:
        load.wait()
    for i in range(row_blocks):
        sk_t[i] = sketch_ref[:, i * order : (i + 1) * order].astype(jnp.float32)
    own = pl.ds(pl.multiple_of(me_c * LANES, LANES), LANES)
    omega = sketch_ref[:, own].astype(jnp.float32)
    rhs = jnp.broadcast_to(rhs_ref[pl.ds(me_c, 1), :], (8, LANES))

    halves = 2
    half = order // halves
    lefts = [
        spread(sk_t, brow_ref[n], bcol_ref[n], col_blocks, col_blocks * width) for n in range(stored)
    ]
    copies = []
    for h in range(halves):
        part = slice(h * half, (h + 1) * half)
        total = jnp.zeros((col_blocks * width, half), jnp.float32)
        for n in range(stored):
            if h == 0:
                loads[n].wait()
            total = total + jnp.dot(lefts[n], vals[n, :, part], preferred_element_type=jnp.float32)
        s_src[h] = total
        if h == 0:
            pl.semaphore_wait(barrier, 2 * cols - 1)
        copies.append(send(s_src.at[h], s_dst.at[h], pair_sem, h, (1 - me_r, me_c)))
    total = jnp.zeros((row_blocks * width, order), jnp.float32)
    for h in range(halves):
        part = slice(h * half, (h + 1) * half)
        copies[h].wait_recv()
        summed = s_src[h] + s_dst[h]
        for j in range(col_blocks):
            scaled = strip(theta_ref, j)[:, part] * summed[j * width : (j + 1) * width]
            zs[h, j] = scaled.astype(jnp.bfloat16).astype(jnp.float32)
        for n in range(stored):
            left = spread(zs.at[h], bcol_ref[n], brow_ref[n], row_blocks, row_blocks * width)
            total = total + dot_nt(left, vals[n, :, part])
    for i in range(row_blocks):
        for p in range(pieces):
            at = pieces * i + p
            y_own[at % 2, at // 2] = total[i * width : (i + 1) * width, p * LANES : (p + 1) * LANES]
    copy = send(y_own.at[1 - core], y_pair, pair_sem, halves, twin)
    copy.wait_recv()
    for t in range(chips):
        y_src[t] = y_own[core, t] + y_pair[t]
    copies = []
    for t in range(1, chips):
        to = lax.rem(chip + t, chips)
        copies.append(send(y_src.at[to], y_dst.at[t], y_sem, t, (me_r, to * 2 + core)))
    y_t = scatter_finish(y_src[chip] + regularize * omega, copies, y_dst)
    y_all[core, chip] = y_t
    gathers = []
    for t in range(1, chips):
        to = lax.rem(chip + t, chips)
        gathers.append(send(y_all.at[core, chip], y_all.at[core, chip], a_sem, t, (me_r, to * 2 + core)))

    both = y_t + precond_shift * omega
    tall_rhs = jnp.broadcast_to(rhs[:1], (width, LANES))
    upper = jnp.concatenate([0.5 * y_t, 0.5 * both], axis=1)
    lower = jnp.concatenate([jnp.zeros((width, LANES), jnp.float32), tall_rhs], axis=1)
    joined = dot_nt(
        jnp.concatenate([both, y_t], axis=1), jnp.concatenate([upper, lower], axis=0), HIGHEST
    )
    packs = LANES // (2 * width)
    tall = width // packs
    packed = jnp.concatenate([joined[s * tall : (s + 1) * tall] for s in range(packs)], axis=1)
    copies = reduce_start(packed, g_plane, g_sem)
    copies = reduce_middle(copies, g_plane, g_depth, g_sem)
    for copy in gathers:
        copy.wait_recv()
    gathered = send(y_all.at[core], y_all.at[core], a_sem, 0, twin)
    summed = reduce_finish(copies, g_depth)
    joined = jnp.concatenate(
        [summed[:, s * 2 * width : (s + 1) * 2 * width] for s in range(packs)], axis=0
    )
    sketched_rhs = joined[:, width : width + 1]
    coeffs, inverse = eliminate(joined)
    coeffs = jnp.broadcast_to(coeffs, (width, LANES))
    taken = jnp.sum(coeffs * y_t, axis=0, keepdims=True)
    direction = (rhs[:1] - taken) / precond_shift

    gathered.wait_recv()
    lines = []
    for i in range(row_blocks):
        taken = []
        for p in range(pieces):
            at = pieces * i + p
            taken.append(jnp.sum(coeffs * y_all[at % 2, at // 2], axis=0, keepdims=True))
        line = (strip(rhs_ref, i) - jnp.concatenate(taken, axis=1)) / precond_shift
        lines.append(line)
        xs[i] = line.astype(jnp.bfloat16).astype(jnp.float32)
    total = jnp.zeros((16, order), jnp.float32)
    for n in range(stored):
        left = spread(xs, brow_ref[n], bcol_ref[n], col_blocks, 16)
        total = total + jnp.dot(left, vals[n], preferred_element_type=jnp.float32)
    e_src[...] = total[:8]
    copy = send(e_src, e_dst, pair_sem, halves + 1, (1 - me_r, me_c))
    weights = jnp.dot(inverse, y_t, precision=HIGHEST)
    copy.wait_recv()
    image_cols = e_src[...] + e_dst[...]
    for j in range(col_blocks):
        line = (strip(theta_ref, j) * image_cols[j : j + 1]).astype(jnp.bfloat16)
        zv[j] = line.astype(jnp.float32)
    total = jnp.zeros((16, order), jnp.float32)
    for n in range(stored):
        left = spread(zv, bcol_ref[n], brow_ref[n], row_blocks, 16)
        total = total + dot_nt(left, vals[n])

    against = regularize * y_t * direction
    curvature = regularize * direction * direction
    for i in range(row_blocks):
        for p in range(pieces):
            part = slice(p * LANES, (p + 1) * LANES)
            piece = total[i : i + 1, part]
            f_src[pieces * i + p, 0:1] = piece
            against = against + y_all[(pieces * i + p) % 2, (pieces * i + p) // 2] * piece
            curvature = curvature + lines[i][:, part] * piece
    at = lax.broadcasted_iota(jnp.int32, (width, LANES), 0)
    diagonal = lax.broadcasted_iota(jnp.int32, (width, LANES), 1) == at
    against = jnp.where(diagonal, jnp.sum(against, axis=1, keepdims=True), 0.0)
    against = jnp.sum(against, axis=0, keepdims=True)
    curvature = jnp.sum(curvature, axis=1, keepdims=True)
    along = jnp.sum(rhs[:1] * direction, axis=1, keepdims=True)
    lane = lax.broadcasted_iota(jnp.int32, (1, LANES), 1)
    value = jnp.where(lane == width, curvature, jnp.where(lane == width + 1, along, against))
    h_src[...] = value
    for to in range(cols):
        f_src[to, 1:2] = value
    copies = []
    for t in range(1, cols):
        to = lax.rem(me_c + t, cols)
        copies.append(send(f_src.at[to], f_dst.at[t], f_sem, t, (me_r, to)))
    crossed = []
    for t in range(cols):
        to = lax.rem(me_c + t, cols)
        crossed.append(send(h_src, h_dst.at[t], h_sem, t, (1 - me_r, to)))
    gathered = scatter_finish(f_src[me_c], copies, f_dst)
    image = gathered[0:1]
    summed = gathered[1:2]
    for t, copy in enumerate(crossed):
        copy.wait_recv()
        summed = summed + h_dst[t]
    alpha = summed[:, width + 1 : width + 2] / summed[:, width : width + 1]
    sketched = jnp.sum(jnp.where(diagonal, summed, 0.0), axis=1, keepdims=True)
    taken = jnp.sum((sketched_rhs - alpha * sketched) * weights, axis=0, keepdims=True)
    out_ref[0:1] = jnp.broadcast_to(alpha, (1, LANES))
    out_ref[1:2] = direction
    out_ref[2:3] = rhs[:1]
    out_ref[3:4] = image
    out_ref[4:5] = taken
    out_ref[5:8] = jnp.zeros((3, LANES), jnp.float32)
    for copy in pending:
        copy.wait_send()


def fused(cols, blocks, block_rows, block_cols, sketch, theta, rhs):
    stored, order = blocks.shape[2], blocks.shape[3]
    local, width = sketch.shape
    row_blocks = local // order
    col_blocks = theta.shape[0] // order
    depth = cols // PLANE
    vmem = pl.BlockSpec(memory_space=pltpu.VMEM)
    hbm = pl.BlockSpec(memory_space=pl.ANY)
    f32, bf16 = jnp.float32, jnp.bfloat16
    reduce_sems = pltpu.SemaphoreType.DMA((2, 2 * PLANE + depth))
    col_sems = pltpu.SemaphoreType.DMA((2, cols))
    out = pl.pallas_call(
        functools.partial(kernel, cols, row_blocks, col_blocks),
        out_shape=jax.ShapeDtypeStruct((8, LANES), jnp.float32),
        in_specs=[hbm] * 6,
        out_specs=vmem,
        scratch_shapes=[
            pltpu.SMEM((stored,), jnp.int32),
            pltpu.SMEM((stored,), jnp.int32),
            pltpu.VMEM((width, local), bf16),
            pltpu.VMEM((theta.shape[0] // LANES, LANES), f32),
            pltpu.VMEM((local // LANES, LANES), f32),
            pltpu.VMEM((stored, order, order), bf16),
            pltpu.VMEM((row_blocks, width, order), f32),
            pltpu.VMEM((2, col_blocks * width, order // 2), f32),
            pltpu.VMEM((2, col_blocks * width, order // 2), f32),
            pltpu.VMEM((2, col_blocks, width, order // 2), f32),
            pltpu.VMEM((2, cols // 2, width, LANES), f32),
            pltpu.VMEM((cols // 2, width, LANES), f32),
            pltpu.VMEM((cols // 2, width, LANES), f32),
            pltpu.VMEM((cols // 2, width, LANES), f32),
            pltpu.VMEM((2, cols // 2, width, LANES), f32),
            pltpu.VMEM((2 * PLANE, 16, LANES), f32),
            pltpu.VMEM((depth, 16, LANES), f32),
            pltpu.VMEM((row_blocks, 1, order), f32),
            pltpu.VMEM((8, order), f32),
            pltpu.VMEM((8, order), f32),
            pltpu.VMEM((col_blocks, 1, order), f32),
            pltpu.VMEM((cols, 2, LANES), f32),
            pltpu.VMEM((cols, 2, LANES), f32),
            pltpu.VMEM((1, LANES), f32),
            pltpu.VMEM((cols, 1, LANES), f32),
            pltpu.SemaphoreType.DMA((stored + 5,)),
            pltpu.SemaphoreType.DMA((2, 4)),
            col_sems,
            col_sems,
            reduce_sems,
            col_sems,
            col_sems,
        ],
        compiler_params=pltpu.CompilerParams(
            collective_id=0, has_side_effects=True, vmem_limit_bytes=VMEM_BYTES
        ),
    )(
        block_rows.reshape(stored),
        block_cols.reshape(stored),
        blocks.reshape(stored, order, order),
        sketch.T,
        theta.reshape(-1, LANES),
        rhs.reshape(-1, LANES),
    )
    alpha, direction, mine, image, taken = (out[i] for i in range(5))
    iterate = alpha * direction
    residual = mine - alpha * image - regularize * iterate
    return iterate, residual, (residual - taken) / precond_shift


def tile_transpose(values, rows_idx, cols_idx, inputs, col_count):
    order = values.shape[1]
    width = inputs.shape[1]
    picked = inputs.reshape(-1, order, width)[rows_idx]
    product = jnp.einsum("nab,nak->nbk", values, picked, preferred_element_type=jnp.float32)
    onehot = (cols_idx[:, None] == jnp.arange(col_count, dtype=jnp.int32)[None, :]).astype(
        jnp.float32
    )
    merged = jnp.einsum("nj,nbk->jbk", onehot, product, precision=lax.Precision.HIGHEST)
    return merged.reshape(col_count * order, width)


def tile_forward(values, rows_idx, cols_idx, inputs, row_count):
    order = values.shape[1]
    width = inputs.shape[1]
    picked = inputs.reshape(-1, order, width)[cols_idx]
    product = jnp.einsum("nab,nbk->nak", values, picked, preferred_element_type=jnp.float32)
    onehot = (rows_idx[:, None] == jnp.arange(row_count, dtype=jnp.int32)[None, :]).astype(
        jnp.float32
    )
    merged = jnp.einsum("ni,nak->iak", onehot, product, precision=lax.Precision.HIGHEST)
    return merged.reshape(row_count * order, width)


def solve_gram(factor, vector):
    middle = lax.linalg.triangular_solve(factor, vector[:, None], left_side=True, lower=True)
    result = lax.linalg.triangular_solve(
        factor, middle, left_side=True, lower=True, transpose_a=True
    )
    return result[:, 0]


def shards(blocks, block_rows, block_cols, sketch, theta, rhs):
    values = blocks[0, 0]
    rows_idx = block_rows[0, 0]
    cols_idx = block_cols[0, 0]
    order = values.shape[1]
    local_rows = sketch.shape[0]
    row_count = local_rows // order
    col_count = theta.shape[0] // order
    share = local_rows // lax.axis_size("col")
    offset = lax.axis_index("col") * share
    sketch_f = sketch.astype(jnp.float32)
    sketch_part = lax.dynamic_slice_in_dim(sketch_f, offset, share, 0)
    rhs_part = lax.dynamic_slice_in_dim(rhs, offset, share, 0)
    col_terms = tile_transpose(values, rows_idx, cols_idx, sketch, col_count)
    sketch_cols = lax.psum(col_terms, "row")
    scaled = (theta[:, None] * sketch_cols).astype(jnp.bfloat16)
    row_terms = tile_forward(values, rows_idx, cols_idx, scaled, row_count)
    ysketch = lax.psum(row_terms, "col") + regularize * sketch_f
    y_part = lax.dynamic_slice_in_dim(ysketch, offset, share, 0)
    cross = jnp.dot(sketch_part.T, y_part, precision=lax.Precision.HIGHEST)
    gram_terms = precond_shift * 0.5 * (cross + cross.T) + jnp.dot(
        y_part.T, y_part, precision=lax.Precision.HIGHEST
    )
    yb_terms = jnp.dot(rhs_part, y_part, precision=lax.Precision.HIGHEST)
    gram, sketched_rhs = lax.psum((gram_terms, yb_terms), ("row", "col"))
    factor = jnp.linalg.cholesky(gram)
    coeffs = solve_gram(factor, sketched_rhs)
    direction_full = (
        rhs - jnp.dot(ysketch, coeffs, precision=lax.Precision.HIGHEST)
    ) / precond_shift
    direction = lax.dynamic_slice_in_dim(direction_full, offset, share, 0)
    dir_low = direction_full.astype(jnp.bfloat16)
    image_terms = tile_transpose(values, rows_idx, cols_idx, dir_low[:, None], col_count)[:, 0]
    image_cols = lax.psum(image_terms, "row")
    image_scaled = (theta * image_cols).astype(jnp.bfloat16)
    product_terms = tile_forward(values, rows_idx, cols_idx, image_scaled[:, None], row_count)[:, 0]
    image_full = lax.psum(product_terms, "col")
    image = lax.dynamic_slice_in_dim(image_full, offset, share, 0) + regularize * direction
    along = lax.psum(jnp.sum(rhs_part * direction), ("row", "col"))
    curvature = lax.psum(jnp.sum(direction * image), ("row", "col"))
    alpha = along / curvature
    residual = rhs_part - alpha * image
    sketched_res = lax.psum(
        jnp.dot(residual, y_part, precision=lax.Precision.HIGHEST), ("row", "col")
    )
    solution = alpha * direction
    res_coeffs = solve_gram(factor, sketched_res)
    precond_residual = (
        residual - jnp.dot(y_part, res_coeffs, precision=lax.Precision.HIGHEST)
    ) / precond_shift
    return (solution, residual, precond_residual)


def solution(mesh):
    in_specs = (
        P("row", "col", None, None, None),
        P("row", "col", None),
        P("row", "col", None),
        P("row", None),
        P("col"),
        P("row"),
    )
    out_specs = (P(("row", "col")), P(("row", "col")), P(("row", "col")))
    cols = mesh.shape["col"]

    def step(blocks, block_rows, block_cols, sketch, theta, rhs):
        share = sketch.shape[0] // cols
        if mesh.shape["row"] == 2 and cols % PLANE == 0 and share == LANES:
            return fused(cols, blocks, block_rows, block_cols, sketch, theta, rhs)
        return shards(blocks, block_rows, block_cols, sketch, theta, rhs)

    return jax.shard_map(step, mesh=mesh, in_specs=in_specs, out_specs=out_specs, check_vma=False)
```

```python
import functools

import jax
import jax.numpy as jnp
from jax import lax
from jax.experimental import pallas as pl
from jax.experimental.pallas import tpu as pltpu
from jax.sharding import PartitionSpec as P

precond_shift = 1.0
regularize = 0.5
MESH = pl.DeviceIdType.MESH
HIGHEST = lax.Precision.HIGHEST
PLANE = 4
LANES = 128
VMEM_BYTES = 64 * 1024 * 1024


def dot_nt(left, right, precision=None):
    return lax.dot_general(
        left, right, (((1,), (1,)), ((), ())), precision=precision, preferred_element_type=jnp.float32
    )


def spread(source, index, place, copies, height):
    picked = source[index]
    width, lanes = picked.shape
    if width == 1:
        tall = jnp.broadcast_to(picked, (height, lanes))
    else:
        tall = jnp.concatenate([picked] * copies, axis=0)
    group = lax.broadcasted_iota(jnp.int32, (height, lanes), 0) // width
    return jnp.where(group == place, tall, 0.0).astype(jnp.bfloat16)


def eliminate(matrix):
    order = matrix.shape[0]
    panel = 8
    at = lax.broadcasted_iota(jnp.int32, (order, LANES), 0)
    lane = lax.broadcasted_iota(jnp.int32, (order, LANES), 1)
    rest = LANES - matrix.shape[1]
    wide = jnp.concatenate([matrix, jnp.zeros((order, rest), jnp.float32)], axis=1)
    wide = jnp.where(lane == at + 2 * order, 1.0, wide)
    for start in range(0, order, panel):
        columns = [
            jnp.broadcast_to(wide[:, k : k + 1], (order, LANES)) for k in range(start, start + panel)
        ]
        for j in range(0, panel, 2):
            k = start + j
            left, right = columns[j], columns[j + 1]
            first = 1.0 / left[k : k + 1]
            ratio = right[k : k + 1] * first
            below = left[k + 1 : k + 2]
            second = 1.0 / (right[k + 1 : k + 2] - below * ratio)

            def clear(target):
                upper = target[k : k + 1] * first
                lower = (target[k + 1 : k + 2] - below * upper) * second
                upper = upper - ratio * lower
                rest = target - left * upper - right * lower
                return jnp.where(at == k, upper, jnp.where(at == k + 1, lower, rest))

            for other in range(j + 2, panel):
                columns[other] = clear(columns[other])
            wide = clear(wide)
    return wide[:, order : order + 1], wide[:, 2 * order : 3 * order]


def kernel(
    cols,
    row_blocks,
    col_blocks,
    brow_hbm,
    bcol_hbm,
    blocks_ref,
    sketch_hbm,
    theta_hbm,
    rhs_hbm,
    out_ref,
    brow_ref,
    bcol_ref,
    sketch_ref,
    theta_ref,
    rhs_ref,
    vals,
    sk_t,
    s_src,
    s_dst,
    zs,
    y_own,
    y_pair,
    y_src,
    y_dst,
    y_all,
    g_plane,
    g_depth,
    xs,
    e_src,
    e_dst,
    zv,
    f_src,
    f_dst,
    h_src,
    h_dst,
    load_sem,
    pair_sem,
    y_sem,
    a_sem,
    g_sem,
    f_sem,
    h_sem,
):
    me_r = lax.axis_index("row")
    me_c = lax.axis_index("col")
    stored, order = vals.shape[0], vals.shape[1]
    width = sketch_ref.shape[0]
    pieces = order // LANES
    depth = cols // PLANE
    z, q = me_c // PLANE, me_c % PLANE
    plane = 2 * PLANE
    me_p = me_r * PLANE + q
    core, chip, chips = lax.rem(me_c, 2), me_c // 2, cols // 2
    twin = (me_r, chip * 2 + 1 - core)
    pending = []

    smalls = []
    for at, (src, dst) in enumerate(
        [
            (sketch_hbm, sketch_ref),
            (brow_hbm, brow_ref),
            (bcol_hbm, bcol_ref),
            (theta_hbm, theta_ref),
            (rhs_hbm, rhs_ref),
        ]
    ):
        load = pltpu.make_async_copy(src, dst, load_sem.at[stored + at])
        load.start()
        smalls.append(load)
    loads = []
    for n in range(stored):
        load = pltpu.make_async_copy(blocks_ref.at[n], vals.at[n], load_sem.at[n])
        load.start()
        loads.append(load)

    barrier = pltpu.get_barrier_semaphore()
    for t in range(1, cols):
        pl.semaphore_signal(
            barrier, inc=1, device_id=(me_r, lax.rem(me_c + t, cols)), device_id_type=MESH
        )
    for t in range(cols):
        pl.semaphore_signal(
            barrier, inc=1, device_id=(1 - me_r, lax.rem(me_c + t, cols)), device_id_type=MESH
        )

    def send(src, dst, sems, at, device):
        copy = pltpu.make_async_remote_copy(
            src_ref=src,
            dst_ref=dst,
            send_sem=sems.at[0, at],
            recv_sem=sems.at[1, at],
            device_id=device,
            device_id_type=MESH,
        )
        copy.start()
        pending.append(copy)
        return copy

    def reduce_start(value, first, sems):
        first[me_p] = value
        copies = []
        for u in range(1, plane):
            peer = lax.rem(me_p + u, plane)
            device = (peer // PLANE, z * PLANE + lax.rem(peer, PLANE))
            copies.append(send(first.at[me_p], first.at[me_p], sems, u - 1, device))
        return copies

    def reduce_middle(copies, first, second, sems):
        for copy in copies:
            copy.wait_recv()
        total = first[0]
        for u in range(1, plane):
            total = total + first[u]
        second[z] = total
        copies = []
        for u in range(1, depth):
            device = (me_r, lax.rem(z + u, depth) * PLANE + q)
            copies.append(send(second.at[z], second.at[z], sems, plane - 2 + u, device))
        return copies

    def reduce_finish(copies, second):
        for copy in copies:
            copy.wait_recv()
        total = second[0]
        for u in range(1, depth):
            total = total + second[u]
        return total

    def scatter_finish(total, copies, dst):
        for t, copy in enumerate(copies, 1):
            copy.wait_recv()
            total = total + dst[t]
        return total

    def strip(ref, j):
        return jnp.concatenate([ref[pieces * j + p : pieces * j + p + 1, :] for p in range(pieces)], axis=1)

    for load in smalls:
        load.wait()
    for i in range(row_blocks):
        sk_t[i] = sketch_ref[:, i * order : (i + 1) * order].astype(jnp.float32)
    own = pl.ds(pl.multiple_of(me_c * LANES, LANES), LANES)
    omega = sketch_ref[:, own].astype(jnp.float32)
    rhs = jnp.broadcast_to(rhs_ref[pl.ds(me_c, 1), :], (8, LANES))

    halves = 2
    half = order // halves
    lefts = [
        spread(sk_t, brow_ref[n], bcol_ref[n], col_blocks, col_blocks * width) for n in range(stored)
    ]
    copies = []
    for h in range(halves):
        part = slice(h * half, (h + 1) * half)
        total = jnp.zeros((col_blocks * width, half), jnp.float32)
        for n in range(stored):
            if h == 0:
                loads[n].wait()
            total = total + jnp.dot(lefts[n], vals[n, :, part], preferred_element_type=jnp.float32)
        s_src[h] = total
        if h == 0:
            pl.semaphore_wait(barrier, 2 * cols - 1)
        copies.append(send(s_src.at[h], s_dst.at[h], pair_sem, h, (1 - me_r, me_c)))
    total = jnp.zeros((row_blocks * width, order), jnp.float32)
    for h in range(halves):
        part = slice(h * half, (h + 1) * half)
        copies[h].wait_recv()
        summed = s_src[h] + s_dst[h]
        for j in range(col_blocks):
            scaled = strip(theta_ref, j)[:, part] * summed[j * width : (j + 1) * width]
            zs[h, j] = scaled.astype(jnp.bfloat16).astype(jnp.float32)
        for n in range(stored):
            left = spread(zs.at[h], bcol_ref[n], brow_ref[n], row_blocks, row_blocks * width)
            total = total + dot_nt(left, vals[n, :, part])
    for i in range(row_blocks):
        for p in range(pieces):
            at = pieces * i + p
            y_own[at % 2, at // 2] = total[i * width : (i + 1) * width, p * LANES : (p + 1) * LANES]
    copy = send(y_own.at[1 - core], y_pair, pair_sem, halves, twin)
    copy.wait_recv()
    for t in range(chips):
        y_src[t] = y_own[core, t] + y_pair[t]
    copies = []
    for t in range(1, chips):
        to = lax.rem(chip + t, chips)
        copies.append(send(y_src.at[to], y_dst.at[t], y_sem, t, (me_r, to * 2 + core)))
    y_t = scatter_finish(y_src[chip] + regularize * omega, copies, y_dst)
    y_all[core, chip] = y_t
    gathers = []
    for t in range(1, chips):
        to = lax.rem(chip + t, chips)
        gathers.append(send(y_all.at[core, chip], y_all.at[core, chip], a_sem, t, (me_r, to * 2 + core)))

    both = y_t + precond_shift * omega
    tall_rhs = jnp.broadcast_to(rhs[:1], (width, LANES))
    upper = jnp.concatenate([0.5 * y_t, 0.5 * both], axis=1)
    lower = jnp.concatenate([jnp.zeros((width, LANES), jnp.float32), tall_rhs], axis=1)
    joined = dot_nt(
        jnp.concatenate([both, y_t], axis=1), jnp.concatenate([upper, lower], axis=0), HIGHEST
    )
    packs = LANES // (2 * width)
    tall = width // packs
    packed = jnp.concatenate([joined[s * tall : (s + 1) * tall] for s in range(packs)], axis=1)
    copies = reduce_start(packed, g_plane, g_sem)
    copies = reduce_middle(copies, g_plane, g_depth, g_sem)
    for copy in gathers:
        copy.wait_recv()
    gathered = send(y_all.at[core], y_all.at[core], a_sem, 0, twin)
    summed = reduce_finish(copies, g_depth)
    joined = jnp.concatenate(
        [summed[:, s * 2 * width : (s + 1) * 2 * width] for s in range(packs)], axis=0
    )
    sketched_rhs = joined[:, width : width + 1]
    coeffs, inverse = eliminate(joined)
    coeffs = jnp.broadcast_to(coeffs, (width, LANES))
    taken = jnp.sum(coeffs * y_t, axis=0, keepdims=True)
    direction = (rhs[:1] - taken) / precond_shift

    gathered.wait_recv()
    lines = []
    for i in range(row_blocks):
        taken = []
        for p in range(pieces):
            at = pieces * i + p
            taken.append(jnp.sum(coeffs * y_all[at % 2, at // 2], axis=0, keepdims=True))
        line = (strip(rhs_ref, i) - jnp.concatenate(taken, axis=1)) / precond_shift
        lines.append(line)
        xs[i] = line.astype(jnp.bfloat16).astype(jnp.float32)
    total = jnp.zeros((16, order), jnp.float32)
    for n in range(stored):
        left = spread(xs, brow_ref[n], bcol_ref[n], col_blocks, 16)
        total = total + jnp.dot(left, vals[n], preferred_element_type=jnp.float32)
    e_src[...] = total[:8]
    copy = send(e_src, e_dst, pair_sem, halves + 1, (1 - me_r, me_c))
    weights = jnp.dot(inverse, y_t, precision=HIGHEST)
    copy.wait_recv()
    image_cols = e_src[...] + e_dst[...]
    for j in range(col_blocks):
        line = (strip(theta_ref, j) * image_cols[j : j + 1]).astype(jnp.bfloat16)
        zv[j] = line.astype(jnp.float32)
    total = jnp.zeros((16, order), jnp.float32)
    for n in range(stored):
        left = spread(zv, bcol_ref[n], brow_ref[n], row_blocks, 16)
        total = total + dot_nt(left, vals[n])

    against = regularize * y_t * direction
    curvature = regularize * direction * direction
    for i in range(row_blocks):
        for p in range(pieces):
            part = slice(p * LANES, (p + 1) * LANES)
            piece = total[i : i + 1, part]
            f_src[pieces * i + p, 0:1] = piece
            against = against + y_all[(pieces * i + p) % 2, (pieces * i + p) // 2] * piece
            curvature = curvature + lines[i][:, part] * piece
    at = lax.broadcasted_iota(jnp.int32, (width, LANES), 0)
    diagonal = lax.broadcasted_iota(jnp.int32, (width, LANES), 1) == at
    against = jnp.where(diagonal, jnp.sum(against, axis=1, keepdims=True), 0.0)
    against = jnp.sum(against, axis=0, keepdims=True)
    curvature = jnp.sum(curvature, axis=1, keepdims=True)
    along = jnp.sum(rhs[:1] * direction, axis=1, keepdims=True)
    lane = lax.broadcasted_iota(jnp.int32, (1, LANES), 1)
    value = jnp.where(lane == width, curvature, jnp.where(lane == width + 1, along, against))
    h_src[...] = value
    for to in range(cols):
        f_src[to, 1:2] = value
    copies = []
    for t in range(1, cols):
        to = lax.rem(me_c + t, cols)
        copies.append(send(f_src.at[to], f_dst.at[t], f_sem, t, (me_r, to)))
    crossed = []
    for t in range(cols):
        to = lax.rem(me_c + t, cols)
        crossed.append(send(h_src, h_dst.at[t], h_sem, t, (1 - me_r, to)))
    gathered = scatter_finish(f_src[me_c], copies, f_dst)
    image = gathered[0:1]
    summed = gathered[1:2]
    for t, copy in enumerate(crossed):
        copy.wait_recv()
        summed = summed + h_dst[t]
    alpha = summed[:, width + 1 : width + 2] / summed[:, width : width + 1]
    sketched = jnp.sum(jnp.where(diagonal, summed, 0.0), axis=1, keepdims=True)
    taken = jnp.sum((sketched_rhs - alpha * sketched) * weights, axis=0, keepdims=True)
    out_ref[0:1] = jnp.broadcast_to(alpha, (1, LANES))
    out_ref[1:2] = direction
    out_ref[2:3] = rhs[:1]
    out_ref[3:4] = image
    out_ref[4:5] = taken
    out_ref[5:8] = jnp.zeros((3, LANES), jnp.float32)
    for copy in pending:
        copy.wait_send()


def fused(cols, blocks, block_rows, block_cols, sketch, theta, rhs):
    stored, order = blocks.shape[2], blocks.shape[3]
    local, width = sketch.shape
    row_blocks = local // order
    col_blocks = theta.shape[0] // order
    depth = cols // PLANE
    vmem = pl.BlockSpec(memory_space=pltpu.VMEM)
    hbm = pl.BlockSpec(memory_space=pl.ANY)
    f32, bf16 = jnp.float32, jnp.bfloat16
    reduce_sems = pltpu.SemaphoreType.DMA((2, 2 * PLANE + depth))
    col_sems = pltpu.SemaphoreType.DMA((2, cols))
    out = pl.pallas_call(
        functools.partial(kernel, cols, row_blocks, col_blocks),
        out_shape=jax.ShapeDtypeStruct((8, LANES), jnp.float32),
        in_specs=[hbm] * 6,
        out_specs=vmem,
        scratch_shapes=[
            pltpu.SMEM((stored,), jnp.int32),
            pltpu.SMEM((stored,), jnp.int32),
            pltpu.VMEM((width, local), bf16),
            pltpu.VMEM((theta.shape[0] // LANES, LANES), f32),
            pltpu.VMEM((local // LANES, LANES), f32),
            pltpu.VMEM((stored, order, order), bf16),
            pltpu.VMEM((row_blocks, width, order), f32),
            pltpu.VMEM((2, col_blocks * width, order // 2), f32),
            pltpu.VMEM((2, col_blocks * width, order // 2), f32),
            pltpu.VMEM((2, col_blocks, width, order // 2), f32),
            pltpu.VMEM((2, cols // 2, width, LANES), f32),
            pltpu.VMEM((cols // 2, width, LANES), f32),
            pltpu.VMEM((cols // 2, width, LANES), f32),
            pltpu.VMEM((cols // 2, width, LANES), f32),
            pltpu.VMEM((2, cols // 2, width, LANES), f32),
            pltpu.VMEM((2 * PLANE, 16, LANES), f32),
            pltpu.VMEM((depth, 16, LANES), f32),
            pltpu.VMEM((row_blocks, 1, order), f32),
            pltpu.VMEM((8, order), f32),
            pltpu.VMEM((8, order), f32),
            pltpu.VMEM((col_blocks, 1, order), f32),
            pltpu.VMEM((cols, 2, LANES), f32),
            pltpu.VMEM((cols, 2, LANES), f32),
            pltpu.VMEM((1, LANES), f32),
            pltpu.VMEM((cols, 1, LANES), f32),
            pltpu.SemaphoreType.DMA((stored + 5,)),
            pltpu.SemaphoreType.DMA((2, 4)),
            col_sems,
            col_sems,
            reduce_sems,
            col_sems,
            col_sems,
        ],
        compiler_params=pltpu.CompilerParams(
            collective_id=0, has_side_effects=True, vmem_limit_bytes=VMEM_BYTES
        ),
    )(
        block_rows.reshape(stored),
        block_cols.reshape(stored),
        blocks.reshape(stored, order, order),
        sketch.T,
        theta.reshape(-1, LANES),
        rhs.reshape(-1, LANES),
    )
    alpha, direction, mine, image, taken = (out[i] for i in range(5))
    iterate = alpha * direction
    residual = mine - alpha * image - regularize * iterate
    return iterate, residual, (residual - taken) / precond_shift


def tile_transpose(values, rows_idx, cols_idx, inputs, col_count):
    order = values.shape[1]
    width = inputs.shape[1]
    picked = inputs.reshape(-1, order, width)[rows_idx]
    product = jnp.einsum("nab,nak->nbk", values, picked, preferred_element_type=jnp.float32)
    onehot = (cols_idx[:, None] == jnp.arange(col_count, dtype=jnp.int32)[None, :]).astype(
        jnp.float32
    )
    merged = jnp.einsum("nj,nbk->jbk", onehot, product, precision=lax.Precision.HIGHEST)
    return merged.reshape(col_count * order, width)


def tile_forward(values, rows_idx, cols_idx, inputs, row_count):
    order = values.shape[1]
    width = inputs.shape[1]
    picked = inputs.reshape(-1, order, width)[cols_idx]
    product = jnp.einsum("nab,nbk->nak", values, picked, preferred_element_type=jnp.float32)
    onehot = (rows_idx[:, None] == jnp.arange(row_count, dtype=jnp.int32)[None, :]).astype(
        jnp.float32
    )
    merged = jnp.einsum("ni,nak->iak", onehot, product, precision=lax.Precision.HIGHEST)
    return merged.reshape(row_count * order, width)


def solve_gram(factor, vector):
    middle = lax.linalg.triangular_solve(factor, vector[:, None], left_side=True, lower=True)
    result = lax.linalg.triangular_solve(
        factor, middle, left_side=True, lower=True, transpose_a=True
    )
    return result[:, 0]


def shards(blocks, block_rows, block_cols, sketch, theta, rhs):
    values = blocks[0, 0]
    rows_idx = block_rows[0, 0]
    cols_idx = block_cols[0, 0]
    order = values.shape[1]
    local_rows = sketch.shape[0]
    row_count = local_rows // order
    col_count = theta.shape[0] // order
    share = local_rows // lax.axis_size("col")
    offset = lax.axis_index("col") * share
    sketch_f = sketch.astype(jnp.float32)
    sketch_part = lax.dynamic_slice_in_dim(sketch_f, offset, share, 0)
    rhs_part = lax.dynamic_slice_in_dim(rhs, offset, share, 0)
    col_terms = tile_transpose(values, rows_idx, cols_idx, sketch, col_count)
    sketch_cols = lax.psum(col_terms, "row")
    scaled = (theta[:, None] * sketch_cols).astype(jnp.bfloat16)
    row_terms = tile_forward(values, rows_idx, cols_idx, scaled, row_count)
    ysketch = lax.psum(row_terms, "col") + regularize * sketch_f
    y_part = lax.dynamic_slice_in_dim(ysketch, offset, share, 0)
    cross = jnp.dot(sketch_part.T, y_part, precision=lax.Precision.HIGHEST)
    gram_terms = precond_shift * 0.5 * (cross + cross.T) + jnp.dot(
        y_part.T, y_part, precision=lax.Precision.HIGHEST
    )
    yb_terms = jnp.dot(rhs_part, y_part, precision=lax.Precision.HIGHEST)
    gram, sketched_rhs = lax.psum((gram_terms, yb_terms), ("row", "col"))
    factor = jnp.linalg.cholesky(gram)
    coeffs = solve_gram(factor, sketched_rhs)
    direction_full = (
        rhs - jnp.dot(ysketch, coeffs, precision=lax.Precision.HIGHEST)
    ) / precond_shift
    direction = lax.dynamic_slice_in_dim(direction_full, offset, share, 0)
    dir_low = direction_full.astype(jnp.bfloat16)
    image_terms = tile_transpose(values, rows_idx, cols_idx, dir_low[:, None], col_count)[:, 0]
    image_cols = lax.psum(image_terms, "row")
    image_scaled = (theta * image_cols).astype(jnp.bfloat16)
    product_terms = tile_forward(values, rows_idx, cols_idx, image_scaled[:, None], row_count)[:, 0]
    image_full = lax.psum(product_terms, "col")
    image = lax.dynamic_slice_in_dim(image_full, offset, share, 0) + regularize * direction
    along = lax.psum(jnp.sum(rhs_part * direction), ("row", "col"))
    curvature = lax.psum(jnp.sum(direction * image), ("row", "col"))
    alpha = along / curvature
    residual = rhs_part - alpha * image
    sketched_res = lax.psum(
        jnp.dot(residual, y_part, precision=lax.Precision.HIGHEST), ("row", "col")
    )
    solution = alpha * direction
    res_coeffs = solve_gram(factor, sketched_res)
    precond_residual = (
        residual - jnp.dot(y_part, res_coeffs, precision=lax.Precision.HIGHEST)
    ) / precond_shift
    return (solution, residual, precond_residual)


def solution(mesh):
    in_specs = (
        P("row", "col", None, None, None),
        P("row", "col", None),
        P("row", "col", None),
        P("row", None),
        P("col"),
        P("row"),
    )
    out_specs = (P(("row", "col")), P(("row", "col")), P(("row", "col")))
    cols = mesh.shape["col"]

    def step(blocks, block_rows, block_cols, sketch, theta, rhs):
        share = sketch.shape[0] // cols
        if mesh.shape["row"] == 2 and cols % PLANE == 0 and share == LANES:
            return fused(cols, blocks, block_rows, block_cols, sketch, theta, rhs)
        return shards(blocks, block_rows, block_cols, sketch, theta, rhs)

    return jax.shard_map(step, mesh=mesh, in_specs=in_specs, out_specs=out_specs, check_vma=False)
```
